512 devices in a mesh: dp: 32 (over y, x, core), tensor: 16 (over z).
Axes of the slice: x: 4, y: 4, z: 16, core: 2. Of those that a mesh axis runs over, the one named last changes fastest.
Arguments:
- ssm_state: float32 [64, 128, 64, 256], P('dp', 'tensor'), may hold values from -6 to 6
- conv_x: float32 [64, 3, 8192], P('dp', None, 'tensor'), may hold values from -6 to 6
- conv_bc: float32 [64, 3, 2048], P('dp'), may hold values from -6 to 6
- x_in: bfloat16 [3, 64, 8192], P(None, 'dp', 'tensor'), may hold values from -6 to 6
- bc_in: bfloat16 [3, 64, 2048], P(None, 'dp'), may hold values from -6 to 6
- z_in: bfloat16 [3, 64, 8192], P(None, 'dp', 'tensor'), may hold values from -6 to 6
- dt_in: bfloat16 [3, 64, 128], P(None, 'dp', 'tensor'), may hold values from -6 to 6
- conv_w_x: float32 [4, 8192], P(None, 'tensor'), may hold values from -3 to 3
- conv_w_bc: float32 [4, 2048], replicated, may hold values from -3 to 3
- dt_bias: float32 [128], P('tensor'), may hold values from -2 to 1
- a_rate: float32 [128], P('tensor'), may hold values from 0.05 to 4
- d_skip: float32 [128], P('tensor'), may hold values from 0.5 to 2
- norm_gain: float32 [8192], P('tensor'), may hold values from 0.1 to 1.9
- send_slot: int32 [3, 32], replicated, may hold values from 0 to 1
- dest_group: int32 [3, 32], replicated, may hold values from 0 to 31, each once within a row
- active: int32 [3, 64], P(None, 'dp'), may hold values 0 or 1
Outputs:
- mixer_out: bfloat16 [3, 64, 8192], P(None, 'dp', 'tensor')
- ssm_final: float32 [64, 128, 64, 256], P('dp', 'tensor')
- conv_x_final: float32 [64, 3, 8192], P('dp', None, 'tensor')
- conv_bc_final: float32 [64, 3, 2048], P('dp')
The draws below stay inside these ranges and needn't reach their ends.
Inputs may be any that keep to these rules, and one draw needn't show every extreme that they name: dest_group[t] is a permutation of the 32 groups for every step t.
All inputs are finite; a program needn't handle non-finite values. No bound on the sum of `active` on one device may be relied on, other than what follows from the above.
Results may differ from the reference program's by a relative error of at most 0.002.
Values sent between devices are 32-bit elements; how exact they have to be, the bound alone decides.
A program may use at most 64 MiB of HBM per device.

```python
import math
import jax
import jax.numpy as jnp
from jax import lax

HEADS = 128
P_SIZE = 64
N = 256
GROUP_HEADS = 32
KERNEL = 4
STEPS = 3
ROW_DEV = 2
GROUPS = 32
ROWS = 64
NG = 4


def set_ends(result, own_key, low, top_value):
    longest = result.shape.index(max(result.shape))
    spots = []
    for shift in (0, 1):
        where = [jax.random.randint(jax.random.fold_in(own_key, axis), (), 0, length) for axis, length in enumerate(result.shape)]
        where[longest] = (where[longest] + shift) % result.shape[longest]
        spots.append(tuple(where))
    return result.at[spots[0]].set(low).at[spots[1]].set(top_value)


def levels(own_key, shape, shards, low, high):
    factor_of = 1.0
    for axis_at, blocks in shards:
        steps = jax.random.uniform(jax.random.fold_in(jax.random.fold_in(own_key, 6), axis_at), (blocks,), jnp.float32, low / len(shards), high / len(shards))
        factor_of = factor_of * jnp.repeat(jnp.exp(steps), shape[axis_at] // blocks).reshape((-1,) + (1,) * (len(shape) - 1 - axis_at))
    return factor_of


def bell_draw(own_key, dims, width, reach, shards=(), kind=jnp.bfloat16):
    entries = jax.random.normal(own_key, dims, jnp.float32) * width
    if len(shards) > 0:
        entries = levels(own_key, dims, shards, -0.22, 0.18) * entries
    return jnp.clip(entries, min=-reach, max=reach).astype(kind)


def setup_inputs(seed: int = 0) -> dict:
    streams_of = jax.random.split(jax.random.key(seed), 17)
    return {
        "ssm_state": bell_draw(streams_of[0], (ROWS, HEADS, P_SIZE, N), 1.0, 6.0, ((0, 32), (1, 16)), jnp.float32),
        "conv_x": bell_draw(streams_of[1], (ROWS, KERNEL - 1, HEADS * P_SIZE), 1.0, 6.0, ((0, 32), (2, 16)), jnp.float32),
        "conv_bc": bell_draw(streams_of[2], (ROWS, KERNEL - 1, 2 * NG * N), 1.0, 6.0, ((0, 32),), jnp.float32),
        "x_in": bell_draw(streams_of[3], (STEPS, ROWS, HEADS * P_SIZE), 1.0, 6.0, ((1, 32), (2, 16))),
        "bc_in": bell_draw(streams_of[4], (STEPS, ROWS, 2 * NG * N), 1.0, 6.0, ((1, 32),)),
        "z_in": bell_draw(streams_of[5], (STEPS, ROWS, HEADS * P_SIZE), 1.0, 6.0, ((1, 32), (2, 16))),
        "dt_in": bell_draw(streams_of[6], (STEPS, ROWS, HEADS), 1.0, 6.0, ((1, 32), (2, 16))),
        "conv_w_x": bell_draw(streams_of[7], (KERNEL, HEADS * P_SIZE), 0.5, 3.0, ((1, 16),), jnp.float32),
        "conv_w_bc": bell_draw(streams_of[8], (KERNEL, 2 * NG * N), 0.5, 3.0, (), jnp.float32),
        "dt_bias": jnp.clip(-2.0 + 3.0 * jax.random.uniform(streams_of[9], (HEADS,), jnp.float32) ** levels(streams_of[9], (HEADS,), ((0, 16),), -0.2, 0.2), -2.0, 1.0),
        "a_rate": jnp.clip(jnp.exp(math.log(4.0) - 4.3820266 * jax.random.uniform(streams_of[10], (HEADS,), jnp.float32) ** levels(streams_of[10], (HEADS,), ((0, 16),), -0.2, 0.2)), 0.05, 4.0),
        "d_skip": jnp.clip(0.5 + 1.5 * jax.random.uniform(streams_of[11], (HEADS,), jnp.float32) ** levels(streams_of[11], (HEADS,), ((0, 16),), -0.2, 0.2), 0.5, 2.0),
        "norm_gain": jnp.clip(1.0 + 0.18 * jax.random.normal(streams_of[12], (HEADS * P_SIZE,), jnp.float32), 0.1, 1.9),
        "send_slot": set_ends(jax.random.randint(streams_of[13], (STEPS, GROUPS), 0, ROW_DEV), jax.random.fold_in(streams_of[13], 1), 0, ROW_DEV - 1).astype(jnp.int32),
        "dest_group": jax.vmap(lambda own: jax.random.permutation(own, GROUPS))(jax.random.split(streams_of[14], STEPS)).reshape((STEPS, GROUPS)).astype(jnp.int32),
        "active": set_ends((jax.random.randint(streams_of[15], (STEPS, ROWS), 0, 4) < 3).astype(jnp.int32), jax.random.fold_in(streams_of[15], 1), 0, 1),
    }


def migrate(values, slots, targets):
    shaped = values.reshape((GROUPS, ROW_DEV) + values.shape[1:])
    groups = jnp.arange(GROUPS, dtype=jnp.int32)
    leaving = shaped[groups, slots]
    anchor = jnp.zeros((GROUPS,), jnp.int32).at[targets].set(groups)
    shaped = shaped.at[groups, slots].set(leaving[anchor])
    return shaped.reshape(values.shape)

def reference(ssm_state, conv_x, conv_bc, x_in, bc_in, z_in, dt_in, conv_w_x, conv_w_bc, dt_bias, a_rate, d_skip, norm_gain, send_slot, dest_group, active):

    def advance_row(items):
        state, state_x, state_bc, x_new, bc_new, z_new, delta_raw, live_row = items
        window_x = jnp.concatenate([state_x, x_new.astype(jnp.float32)[None]], 0)
        window_bc = jnp.concatenate([state_bc, bc_new.astype(jnp.float32)[None]], 0)
        mixed_x = jax.nn.silu(lax.optimization_barrier(jnp.sum(window_x * conv_w_x, 0))).reshape(HEADS, P_SIZE)
        mixed_bc = jax.nn.silu(lax.optimization_barrier(jnp.sum(window_bc * conv_w_bc, 0))).reshape(2, HEADS // GROUP_HEADS, N)
        b_heads = jnp.repeat(mixed_bc[0], GROUP_HEADS, axis=0)
        c_heads = jnp.repeat(mixed_bc[1], GROUP_HEADS, axis=0)
        delta = jax.nn.softplus(delta_raw.astype(jnp.float32) + dt_bias)
        decay = jnp.exp(-delta * a_rate)
        fresh = decay[:, None, None] * state + (delta[:, None] * mixed_x)[:, :, None] * b_heads[:, None, :]
        read = jnp.einsum('hpn,hn->hp', fresh, c_heads, precision=lax.Precision.HIGHEST) + d_skip[:, None] * mixed_x
        gated = read.reshape(HEADS * P_SIZE) * jax.nn.silu(z_new.astype(jnp.float32))
        grouped = gated.reshape(HEADS // GROUP_HEADS, GROUP_HEADS * P_SIZE)
        factor = lax.rsqrt(lax.optimization_barrier(jnp.mean(grouped * grouped, 1)) + 1e-05)
        normed = (grouped * factor[:, None]).reshape(HEADS * P_SIZE) * norm_gain
        live = live_row > 0
        output = jnp.where(live, normed, 0.0).astype(jnp.bfloat16)
        return (output, jnp.where(live, fresh, state), jnp.where(live, window_x[1:], state_x), jnp.where(live, window_bc[1:], state_bc))
    outputs = []
    for turn in range(STEPS):
        ssm_state = migrate(ssm_state, send_slot[turn], dest_group[turn])
        conv_x = migrate(conv_x, send_slot[turn], dest_group[turn])
        conv_bc = migrate(conv_bc, send_slot[turn], dest_group[turn])
        output, ssm_state, conv_x, conv_bc = lax.map(advance_row, (ssm_state, conv_x, conv_bc, x_in[turn], bc_in[turn], z_in[turn], dt_in[turn], active[turn]))
        outputs.append(output)
    return (jnp.stack(outputs, 0), ssm_state, conv_x, conv_bc)
```

```python
import jax
import jax.numpy as jnp
from jax import lax
from jax.experimental import pallas as pl
from jax.experimental.pallas import tpu as pltpu
from jax.sharding import PartitionSpec as P

MESH = pl.DeviceIdType.MESH
HIGH = lax.Precision.HIGHEST
STEPS = 3
SIDE = 4
CHIPS = 16
PLANE = 32
ROWS = 64
CHUNK = 32
HALF = 128
TENSOR = 16
GROUPS = 4
NORM_WIDTH = 2048

HOPS = (
    (2, 2), (2, 1), (1, 2), (2, 3), (3, 2), (2, 0), (0, 2), (1, 1),
    (3, 3), (1, 3), (3, 1), (1, 0), (0, 1), (3, 0), (0, 3), (0, 0),
)
OFFSETS = tuple(
    (kc, kx, ky) for kx, ky in HOPS for kc in (0, 1) if (kc, kx, ky) != (0, 0, 0)
)


def dot_nt(a, b, precision=HIGH):
    return lax.dot_general(
        a, b, (((1,), (1,)), ((), ())), precision=precision,
        preferred_element_type=jnp.float32,
    )


def dot_nn(a, b, precision=HIGH):
    return lax.dot_general(
        a, b, (((1,), (0,)), ((), ())), precision=precision,
        preferred_element_type=jnp.float32,
    )


def silu(v):
    return v / (1.0 + jnp.exp(-v))


def column(row_values, same):
    return jnp.sum(jnp.where(same, row_values, 0.0), axis=1, keepdims=True)


def kernel(
    ssm, bcp, xp, zp, dest, send, w16, wbc, dt_bias, a_rate, d_skip,
    out_s, out_g, out_tot, out_bc,
    pk, buf, sbuf, obuf, dxs, decs, mixed, hists, flat, ysend, yrecv,
    bcsend, bcrecv, sqsend, sqrecv, sidx_v, sidx_s,
    pk_ss, pk_rs, s_ss, s_rs, o_ss, o_rs, y_ss, y_rs, b_ss, b_rs, q_ss, q_rs, local_sem,
):
    d = lax.axis_index("dp")
    z = lax.axis_index("tensor")
    c = d % 2
    q = d // 2
    x = q % SIDE
    y = q // SIDE
    g = z // SIDE
    m = z % SIDE

    def at(offset):
        kc, kx, ky = offset
        cc = (c + kc) % 2
        qq = ((y + ky) % SIDE) * SIDE + (x + kx) % SIDE
        return qq * 2 + cc, qq, cc

    bc_peers = [
        (i, cc, (q * 2 + (c + cc) % 2, ((g + i) % GROUPS) * SIDE + m))
        for i in range(GROUPS)
        for cc in range(2)
        if (i, cc) != (0, 0)
    ]
    norm_peers = [(d, g * SIDE + (m + i) % SIDE) for i in range(1, SIDE)]

    barrier = pltpu.get_barrier_semaphore()
    signals = 0
    for offset in OFFSETS:
        pl.semaphore_signal(barrier, inc=1, device_id=(at(offset)[0], z), device_id_type=MESH)
        signals += 1
    for i, cc, peer in bc_peers:
        if i:
            pl.semaphore_signal(barrier, inc=1, device_id=peer, device_id_type=MESH)
            signals += 1
    for peer in norm_peers:
        pl.semaphore_signal(barrier, inc=1, device_id=peer, device_id_type=MESH)
        signals += 1

    def fill(qq, _):
        for cc in range(2):
            j = qq * 2 + cc
            for h in range(2):
                pk[j, h] = bcp[cc, h]
                pk[j, h, 6:7, :] = xp[qq, 0:1, HALF * h : HALF * (h + 1)]
                pk[j, h, 14:15, :] = xp[qq, 1:2, HALF * h : HALF * (h + 1)]
        return 0

    lax.fori_loop(0, CHIPS, fill, 0)
    pl.semaphore_wait(barrier, signals)

    def rows_of(device):
        return pl.ds(pl.multiple_of(device * 2, 2), 2)

    def small_copy(offset):
        p, _, _ = at(offset)
        return pltpu.make_async_remote_copy(
            src_ref=pk.at[p],
            dst_ref=buf.at[:, pl.ds(pl.multiple_of(d * 16, 16), 16)],
            send_sem=pk_ss.at[p], recv_sem=pk_rs.at[d],
            device_id=(p, z), device_id_type=MESH,
        )

    def small_arrival(p):
        return pltpu.make_async_remote_copy(
            src_ref=pk.at[p],
            dst_ref=buf.at[:, pl.ds(pl.multiple_of(p * 16, 16), 16)],
            send_sem=pk_ss.at[p], recv_sem=pk_rs.at[p],
            device_id=(p, z), device_id_type=MESH,
        )

    def slab(qq, cc):
        return (
            slice(None),
            pl.ds(pl.multiple_of(qq * CHUNK, CHUNK), CHUNK),
            pl.ds(pl.multiple_of(cc * HALF, HALF), HALF),
        )

    def state_copy(p, qq, cc, source):
        return pltpu.make_async_remote_copy(
            src_ref=ssm.at[slab(qq, cc)],
            dst_ref=sbuf.at[rows_of(source)],
            send_sem=s_ss.at[p], recv_sem=s_rs.at[source],
            device_id=(p, z), device_id_type=MESH,
        )

    own_small = pltpu.make_async_copy(
        pk.at[d], buf.at[:, pl.ds(pl.multiple_of(d * 16, 16), 16)], local_sem.at[0]
    )
    own_state = pltpu.make_async_copy(
        ssm.at[slab(q, c)], sbuf.at[rows_of(d)], local_sem.at[1]
    )
    for offset in OFFSETS:
        small_copy(offset).start()
    own_small.start()
    for offset in OFFSETS:
        p, qq, cc = at(offset)
        state_copy(p, qq, cc, d).start()
    own_state.start()

    down = lax.broadcasted_iota(jnp.int32, (ROWS, ROWS), 0)
    across = lax.broadcasted_iota(jnp.int32, (ROWS, ROWS), 1)
    same = down == across
    eye = same.astype(jnp.float32)
    moves = []
    picks = []
    for t in range(STEPS):
        dest_row = dest[t : t + 1, :]
        send_row = send[t : t + 1, :]
        send_col = jnp.sum(jnp.where(same, send_row, 0), axis=1, keepdims=True)
        arrives = (dest_row == down // 2) & (send_row == across % 2)
        moved = send_col == down % 2
        picks.append((moved & arrives) | (jnp.logical_not(moved) & same))
        moves.append(picks[t].astype(jnp.float32).astype(jnp.bfloat16))
    place2 = moves[2].astype(jnp.float32)
    place1 = dot_nn(moves[2], moves[1], None)
    place0 = dot_nn(place1.astype(jnp.bfloat16), moves[0], None)
    source = jnp.sum(jnp.where(picks[2], across, 0), axis=1, keepdims=True)
    for t in (1, 0):
        before = jnp.sum(jnp.where(picks[t], across, 0), axis=1, keepdims=True)
        before = jnp.sum(jnp.where(same, before, 0), axis=0, keepdims=True)
        source = jnp.sum(jnp.where(across == source, before, 0), axis=1, keepdims=True)
    source = jnp.sum(jnp.where(same, source, 0), axis=0, keepdims=True)
    source = jnp.minimum(jnp.maximum(source, 0), ROWS - 1)
    sidx_v[:, 0:ROWS] = jnp.broadcast_to(source, (8, ROWS))
    sidx_v[:, ROWS:] = jnp.zeros((8, ROWS), jnp.int32)
    to_scalar = pltpu.make_async_copy(sidx_v, sidx_s, local_sem.at[2])
    to_scalar.start()
    places = (place1, place2, eye)

    own_small.wait()
    for offset in OFFSETS:
        small_arrival(at(offset)[0]).wait_recv()

    def entry(e):
        return jnp.concatenate(
            [buf[h, pl.ds(e, ROWS, stride=8), :] for h in range(2)], axis=1
        )

    packed = entry(6)
    turned = jnp.transpose(packed)
    first = dot_nt(turned, place0)
    later = (dot_nt(turned, place1), dot_nt(turned, place2), turned)
    window = [first[CHUNK * k : CHUNK * (k + 1)] for k in range(3)]
    pick = (
        lax.broadcasted_iota(jnp.int32, (CHUNK, HALF), 0)
        == lax.broadcasted_iota(jnp.int32, (CHUNK, HALF), 1)
    ).astype(jnp.float32)
    weights = dot_nt(pick, w16[q])
    head = q // 2
    bias = dt_bias[head]
    rate = a_rate[head]
    skip = jnp.where(c == 0, d_skip[head], 0.0)
    live_cols = []
    skipped = []
    for t in range(STEPS):
        new = later[t][96 + CHUNK * t : 96 + CHUNK * (t + 1)]
        raw = later[t][192 + t : 193 + t] + bias
        live = later[t][195 + t : 196 + t]
        delta = jnp.maximum(raw, 0.0) + jnp.log1p(jnp.exp(-jnp.abs(raw)))
        decay = jnp.exp(-delta * rate)
        mixed_x = silu(
            window[0] * weights[:, 0:1]
            + window[1] * weights[:, 1:2]
            + window[2] * weights[:, 2:3]
            + new * weights[:, 3:4]
        )
        on = jnp.broadcast_to(live, (CHUNK, ROWS)) > 0.5
        dxs[t, :, 0:ROWS] = jnp.where(on, delta * mixed_x, 0.0)
        decs[t, :, 0:ROWS] = jnp.broadcast_to(
            jnp.where(live > 0.5, decay, 1.0), (8, ROWS)
        )
        skipped.append(skip * mixed_x)
        window = [
            jnp.where(on, window[1], window[0]),
            jnp.where(on, window[2], window[1]),
            jnp.where(on, new, window[2]),
        ]
        live_cols.append(column(live, same))

    window_bc = [dot_nn(place0, entry(e)) for e in range(3)]
    base = g * 2 * HALF + c * HALF
    w_b = wbc[:, pl.ds(pl.multiple_of(base, HALF), HALF)]
    w_c = wbc[:, pl.ds(pl.multiple_of(base + 1024, HALF), HALF)]
    w_bc = jnp.concatenate([w_b, w_c], axis=1)
    for t in range(STEPS):
        new = entry(3 + t)
        if t < 2:
            new = dot_nn(places[t], new)
        both = silu(
            window_bc[0] * w_bc[0:1]
            + window_bc[1] * w_bc[1:2]
            + window_bc[2] * w_bc[2:3]
            + new * w_bc[3:4]
        )
        mixed[t, 0] = both[:, :HALF]
        mixed[t, 1] = both[:, HALF:]
        on = jnp.broadcast_to(live_cols[t], (ROWS, 2 * HALF)) > 0.5
        window_bc = [
            jnp.where(on, window_bc[1], window_bc[0]),
            jnp.where(on, window_bc[2], window_bc[1]),
            jnp.where(on, new, window_bc[2]),
        ]
    for e in range(3):
        for h in range(2):
            hists[e, h] = window_bc[e][:, HALF * h : HALF * (h + 1)]

    def slot_row(e, h, cc, j):
        return hists[e, h, pl.ds(q * 4 + cc * 2 + j, 1), :]

    for shift in range(2):
        cc = (c + shift) % 2
        bcsend[shift] = jnp.zeros((8, 2 * HALF), jnp.float32)
        for e in range(3):
            for j in range(2):
                for h in range(2):
                    bcsend[
                        shift, e * 2 + j : e * 2 + j + 1, HALF * h : HALF * (h + 1)
                    ] = slot_row(e, h, cc, j)
    bc_copies = []
    for n, (i, shift, peer) in enumerate(bc_peers):
        copy = pltpu.make_async_remote_copy(
            src_ref=bcsend.at[shift], dst_ref=bcrecv.at[g * 2 + c],
            send_sem=b_ss.at[n], recv_sem=b_rs.at[n],
            device_id=peer, device_id_type=MESH,
        )
        copy.start()
        bc_copies.append(copy)
    own_bc = pltpu.make_async_copy(bcsend.at[0], bcrecv.at[g * 2 + c], local_sem.at[3])
    own_bc.start()

    to_scalar.wait()
    own_state.wait()
    for offset in OFFSETS:
        p, qq, cc = at(offset)
        state_copy(p, qq, cc, p).wait_recv()

    lane = lax.broadcasted_iota(jnp.int32, (CHUNK, HALF), 1)
    lane8 = lax.broadcasted_iota(jnp.int32, (8, HALF), 1)

    def advance(f, ys):
        state = sbuf[sidx_s[0, f]].reshape(4, 8, HALF)
        here = lane == f
        here8 = lane8 == f
        reads = []
        for t in range(STEPS):
            dx = jnp.sum(jnp.where(here, dxs[t], 0.0), axis=1, keepdims=True)
            dec = jnp.sum(jnp.where(here8, decs[t], 0.0), axis=1, keepdims=True)
            b_row = mixed[t, 0, pl.ds(f, 1), :]
            c_row = mixed[t, 1, pl.ds(f, 1), :]
            state = state * dec[None] + (dx * b_row).reshape(4, 8, HALF)
            read = jnp.sum(
                state.reshape(CHUNK, HALF) * c_row, axis=1, keepdims=True
            )
            reads.append(jnp.where(here, read, ys[t]))
        obuf[f] = state.reshape(CHUNK, HALF)
        return tuple(reads)

    def advance_some(i, ys):
        for k in range(4):
            ys = advance(i * 4 + k, ys)
        return ys

    zero = jnp.zeros((CHUNK, HALF), jnp.float32)
    ys = lax.fori_loop(0, ROWS // 4, advance_some, (zero,) * STEPS)

    pieces = [None] * 6
    for t in range(STEPS):
        read = ys[t][:, 0:ROWS] + skipped[t]
        back = eye if t == 2 else dot_nt(eye, places[t])
        pieces[t] = dot_nt(back, read)
        pieces[3 + t] = dot_nt(eye, window[t])
    for n in range(6):
        lo = CHUNK * (n % 4)
        flat[n // 4, :, lo : lo + CHUNK] = pieces[n]
    flat[1, :, 2 * CHUNK :] = jnp.zeros((ROWS, 2 * CHUNK), jnp.float32)

    def spread_rows(j, _):
        for n in range(2):
            for h in range(2):
                ysend[j, n : n + 1, HALF * h : HALF * (h + 1)] = flat[
                    h, pl.ds(j * 2 + n, 1), :
                ]
        return 0

    lax.fori_loop(0, PLANE, spread_rows, 0)

    def read_copy(p, source):
        return pltpu.make_async_remote_copy(
            src_ref=ysend.at[p], dst_ref=yrecv.at[source],
            send_sem=y_ss.at[p], recv_sem=y_rs.at[source],
            device_id=(p, z), device_id_type=MESH,
        )

    def final_copy(p, qq, cc, source):
        return pltpu.make_async_remote_copy(
            src_ref=obuf.at[rows_of(p)], dst_ref=out_s.at[slab(qq, cc)],
            send_sem=o_ss.at[p], recv_sem=o_rs.at[source],
            device_id=(p, z), device_id_type=MESH,
        )

    own_read = pltpu.make_async_copy(ysend.at[d], yrecv.at[d], local_sem.at[4])
    own_final = pltpu.make_async_copy(
        obuf.at[rows_of(d)], out_s.at[slab(q, c)], local_sem.at[5]
    )
    for offset in OFFSETS:
        read_copy(at(offset)[0], d).start()
    own_read.start()
    for offset in OFFSETS:
        final_copy(at(offset)[0], q, c, d).start()
    own_final.start()

    own_read.wait()
    for offset in OFFSETS:
        p = at(offset)[0]
        read_copy(p, p).wait_recv()
    lane2 = lax.broadcasted_iota(jnp.int32, (2, 2 * HALF), 1)
    total = jnp.zeros((2, 2 * HALF), jnp.float32)
    for qq in range(CHIPS):
        read = yrecv[2 * qq] + jnp.where(lane2 < 96, yrecv[2 * qq + 1], 0.0)
        gated = read * silu(zp[qq])
        out_g[qq] = jnp.where(lane2 < 96, gated, read)
        total = total + gated * gated
    fold = (
        lax.broadcasted_iota(jnp.int32, (2 * HALF, HALF), 0) // CHUNK
        == lax.broadcasted_iota(jnp.int32, (2 * HALF, HALF), 1)
    ).astype(jnp.float32)
    sqsend[...] = jnp.zeros((8, HALF), jnp.float32)
    sqsend[0:2, :] = dot_nn(total, fold)
    sq_copies = []
    for n, peer in enumerate(norm_peers):
        copy = pltpu.make_async_remote_copy(
            src_ref=sqsend, dst_ref=sqrecv.at[n],
            send_sem=q_ss.at[n], recv_sem=q_rs.at[n],
            device_id=peer, device_id_type=MESH,
        )
        copy.start()
        sq_copies.append(copy)
    for copy in bc_copies:
        copy.wait()
    own_bc.wait()
    out_bc[...] = bcrecv[...]
    for copy in sq_copies:
        copy.wait()
    out_tot[...] = sqsend[...] + sqrecv[0] + sqrecv[1] + sqrecv[2]

    own_final.wait()
    for offset in OFFSETS:
        p, qq, cc = at(offset)
        final_copy(p, qq, cc, p).wait_recv()
    for offset in OFFSETS:
        p, qq, cc = at(offset)
        small_copy(offset).wait_send()
        state_copy(p, qq, cc, d).wait_send()
        read_copy(p, d).wait_send()
        final_copy(p, q, c, d).wait_send()


def local(
    ssm_state, conv_x, conv_bc, x_in, bc_in, z_in, dt_in, conv_w_x, conv_w_bc,
    dt_bias, a_rate, d_skip, norm_gain, send_slot, dest_group, active,
):
    f32 = jnp.float32
    g = lax.axis_index("tensor") // SIDE

    bc_all = jnp.concatenate([conv_bc, jnp.swapaxes(bc_in, 0, 1).astype(f32)], axis=1)
    bc_all = lax.dynamic_index_in_dim(
        bc_all.reshape(2, 6, 2, GROUPS, 2, HALF), g, 3, keepdims=False
    )
    bcp = jnp.transpose(bc_all, (3, 2, 0, 1, 4))
    bcp = jnp.pad(bcp, ((0, 0),) * 3 + ((0, 2), (0, 0))).reshape(2, 2, 16, HALF)

    x_all = jnp.concatenate([conv_x, jnp.swapaxes(x_in, 0, 1).astype(f32)], axis=1)
    x_all = jnp.transpose(x_all.reshape(2, 6, CHIPS, CHUNK), (2, 0, 1, 3))
    dt_all = jnp.repeat(jnp.transpose(dt_in.astype(f32), (2, 1, 0)), 2, axis=0)
    live = jnp.broadcast_to(jnp.transpose(active).astype(f32)[None], (CHIPS, 2, STEPS))
    xp = jnp.concatenate(
        [x_all.reshape(CHIPS, 2, 192), dt_all, live, jnp.zeros((CHIPS, 2, 58), f32)],
        axis=2,
    )
    zp = jnp.transpose(z_in.astype(f32).reshape(STEPS, 2, CHIPS, CHUNK), (2, 1, 0, 3))
    zp = jnp.pad(zp.reshape(CHIPS, 2, 96), ((0, 0), (0, 0), (0, 160)))
    w16 = jnp.transpose(conv_w_x.reshape(4, CHIPS, CHUNK), (1, 0, 2))
    w16 = jnp.pad(w16, ((0, 0), (0, 4), (0, HALF - CHUNK)))
    dest2 = jnp.repeat(dest_group, 2, axis=1)
    send2 = jnp.repeat(send_slot, 2, axis=1)

    vmem = pl.BlockSpec(memory_space=pltpu.VMEM)
    smem = pl.BlockSpec(memory_space=pltpu.SMEM)
    hbm = pl.BlockSpec(memory_space=pl.ANY)
    dma = pltpu.SemaphoreType.DMA
    out_s, out_g, out_tot, out_bc = pl.pallas_call(
        kernel,
        out_shape=(
            jax.ShapeDtypeStruct((2, 512, 256), f32),
            jax.ShapeDtypeStruct((CHIPS, 2, 256), f32),
            jax.ShapeDtypeStruct((8, HALF), f32),
            jax.ShapeDtypeStruct((8, 8, 256), f32),
        ),
        in_specs=[hbm] + [vmem] * 7 + [smem] * 3,
        out_specs=(hbm, vmem, vmem, vmem),
        scratch_shapes=[
            pltpu.VMEM((PLANE, 2, 16, HALF), f32),
            pltpu.VMEM((2, PLANE * 16, HALF), f32),
            pltpu.VMEM((ROWS, CHUNK, HALF), f32),
            pltpu.VMEM((ROWS, CHUNK, HALF), f32),
            pltpu.VMEM((STEPS, CHUNK, HALF), f32),
            pltpu.VMEM((STEPS, 8, HALF), f32),
            pltpu.VMEM((STEPS, 2, ROWS, HALF), f32),
            pltpu.VMEM((3, 2, ROWS, HALF), f32),
            pltpu.VMEM((2, ROWS, HALF), f32),
            pltpu.VMEM((PLANE, 2, 256), f32),
            pltpu.VMEM((PLANE, 2, 256), f32),
            pltpu.VMEM((2, 8, 256), f32),
            pltpu.VMEM((8, 8, 256), f32),
            pltpu.VMEM((8, HALF), f32),
            pltpu.VMEM((3, 8, HALF), f32),
            pltpu.VMEM((8, HALF), jnp.int32),
            pltpu.SMEM((8, HALF), jnp.int32),
            dma((PLANE,)), dma((PLANE,)),
            dma((PLANE,)), dma((PLANE,)),
            dma((PLANE,)), dma((PLANE,)),
            dma((PLANE,)), dma((PLANE,)),
            dma((8,)), dma((8,)),
            dma((4,)), dma((4,)),
            dma((8,)),
        ],
        compiler_params=pltpu.CompilerParams(
            collective_id=0, has_side_effects=True, vmem_limit_bytes=48 * 2**20
        ),
    )(
        ssm_state.reshape(2, 512, 256), bcp, xp, zp, dest2, send2, w16, conv_w_bc,
        dt_bias, a_rate, d_skip,
    )

    factor = lax.rsqrt(out_tot[0:2, 0:STEPS] / NORM_WIDTH + 1e-05)
    packed = out_g[:, :, 0:192].reshape(CHIPS, 2, 6, CHUNK)
    normed = (
        packed[:, :, 0:3] * factor[None, :, :, None]
        * norm_gain.reshape(CHIPS, 1, 1, CHUNK)
    )
    normed = jnp.where(jnp.transpose(active)[None, :, :, None] > 0, normed, 0.0)
    mixer = jnp.transpose(normed.astype(jnp.bfloat16), (2, 1, 0, 3)).reshape(STEPS, 2, 512)
    final_x = jnp.transpose(packed[:, :, 3:6], (1, 2, 0, 3)).reshape(2, 3, 512)
    final_bc = out_bc[:, 0:6].reshape(GROUPS, 2, 3, 2, 2, HALF)
    final_bc = jnp.transpose(final_bc, (3, 2, 4, 0, 1, 5)).reshape(2, 3, 2048)
    return mixer, out_s.reshape(ssm_state.shape), final_x, final_bc


def solution(mesh):
    return jax.shard_map(
        local,
        mesh=mesh,
        in_specs=(
            P("dp", "tensor", None, None),
            P("dp", None, "tensor"),
            P("dp", None, None),
            P(None, "dp", "tensor"),
            P(None, "dp", None),
            P(None, "dp", "tensor"),
            P(None, "dp", "tensor"),
            P(None, "tensor"),
            P(),
            P("tensor"),
            P("tensor"),
            P("tensor"),
            P("tensor"),
            P(),
            P(),
            P(None, "dp"),
        ),
        out_specs=(
            P(None, "dp", "tensor"),
            P("dp", "tensor", None, None),
            P("dp", None, "tensor"),
            P("dp", None, None),
        ),
        check_vma=False,
    )
```

```python
import jax
import jax.numpy as jnp
from jax import lax
from jax.experimental import pallas as pl
from jax.experimental.pallas import tpu as pltpu
from jax.sharding import PartitionSpec as P

MESH = pl.DeviceIdType.MESH
HIGH = lax.Precision.HIGHEST
STEPS = 3
SIDE = 4
CHIPS = 16
PLANE = 32
ROWS = 64
CHUNK = 32
PARTS = 2
PART = CHUNK // PARTS
HALF = 128
TENSOR = 16
GROUPS = 4
NORM_WIDTH = 2048

HOPS = (
    (2, 2), (2, 1), (1, 2), (2, 3), (3, 2), (2, 0), (0, 2), (1, 1),
    (3, 3), (1, 3), (3, 1), (1, 0), (0, 1), (3, 0), (0, 3), (0, 0),
)
OFFSETS = tuple(
    (kc, kx, ky) for kx, ky in HOPS for kc in (0, 1) if (kc, kx, ky) != (0, 0, 0)
)


def dot_nt(a, b, precision=HIGH):
    return lax.dot_general(
        a, b, (((1,), (1,)), ((), ())), precision=precision,
        preferred_element_type=jnp.float32,
    )


def dot_nn(a, b, precision=HIGH):
    return lax.dot_general(
        a, b, (((1,), (0,)), ((), ())), precision=precision,
        preferred_element_type=jnp.float32,
    )


def silu(v):
    return v / (1.0 + jnp.exp(-v))


def column(row_values, same):
    return jnp.sum(jnp.where(same, row_values, 0.0), axis=1, keepdims=True)


def kernel(
    ssm, bcp, bcx, xp, zp, dest, send, w16, wbc, dt_bias, a_rate, d_skip,
    out_s, out_g, out_tot,
    pk, buf, sbuf0, sbuf1, obuf, dxs, decs, mixed, flat, ysend, yrecv,
    sqsend, sqrecv, sidx_v, wbc_v, sidx_s,
    w_sem, pk_ss, pk_rs, s_ss, s_rs, o_ss, o_rs, y_ss, y_rs, q_ss, q_rs, local_sem,
):
    sbufs = (sbuf0, sbuf1)
    d = lax.axis_index("dp")
    z = lax.axis_index("tensor")
    c = d % 2
    q = d // 2
    x = q % SIDE
    y = q // SIDE
    g = z // SIDE
    m = z % SIDE

    def at(offset):
        kc, kx, ky = offset
        cc = (c + kc) % 2
        qq = ((y + ky) % SIDE) * SIDE + (x + kx) % SIDE
        return qq * 2 + cc, qq, cc

    norm_peers = [(d, g * SIDE + (m + i) % SIDE) for i in range(1, SIDE)]

    barrier = pltpu.get_barrier_semaphore()
    signals = 0
    for offset in OFFSETS:
        pl.semaphore_signal(barrier, inc=1, device_id=(at(offset)[0], z), device_id_type=MESH)
        signals += 1
    for peer in norm_peers:
        pl.semaphore_signal(barrier, inc=1, device_id=peer, device_id_type=MESH)
        signals += 1

    w_copies = []
    for h in range(2):
        base = pl.multiple_of(h * 1024 + g * 2 * HALF + c * HALF, HALF)
        w_copies.append(
            pltpu.make_async_copy(wbc.at[:, pl.ds(base, HALF)], wbc_v.at[h], w_sem.at[h])
        )
        w_copies[h].start()

    def fill(qq, _):
        for cc in range(2):
            p = qq * 2 + cc
            for j in range(2):
                for h in range(2):
                    pk[p, j * 2 + h] = bcp[cc, j, h]
                    pk[p, j * 2 + h, 6:7, :] = xp[qq, j : j + 1, HALF * h : HALF * (h + 1)]
            pk[p, 4] = bcx[p]
        return 0

    lax.fori_loop(0, CHIPS, fill, 0)
    pl.semaphore_wait(barrier, signals)

    def lines(device):
        return pl.ds(pl.multiple_of(device * 8, 8), 8)

    def small_copy(p, source):
        return pltpu.make_async_remote_copy(
            src_ref=pk.at[p], dst_ref=buf.at[:, lines(source)],
            send_sem=pk_ss.at[p], recv_sem=pk_rs.at[source],
            device_id=(p, z), device_id_type=MESH,
        )

    def slab(qq, cc, part):
        return (
            slice(None),
            pl.ds(pl.multiple_of(qq * CHUNK + part * PART, PART), PART),
            pl.ds(pl.multiple_of(cc * HALF, HALF), HALF),
        )

    def state_copy(p, qq, cc, part, source):
        return pltpu.make_async_remote_copy(
            src_ref=ssm.at[slab(qq, cc, part)],
            dst_ref=sbufs[part].at[:, source],
            send_sem=s_ss.at[part, p], recv_sem=s_rs.at[part, source],
            device_id=(p, z), device_id_type=MESH,
        )

    own_small = pltpu.make_async_copy(pk.at[d], buf.at[:, lines(d)], local_sem.at[0])
    own_states = [
        pltpu.make_async_copy(
            ssm.at[slab(q, c, part)], sbufs[part].at[:, d], local_sem.at[1 + part]
        )
        for part in range(PARTS)
    ]
    for offset in OFFSETS:
        small_copy(at(offset)[0], d).start()
    own_small.start()
    for part in range(PARTS):
        for offset in OFFSETS:
            p, qq, cc = at(offset)
            state_copy(p, qq, cc, part, d).start()
        own_states[part].start()

    down = lax.broadcasted_iota(jnp.int32, (ROWS, ROWS), 0)
    across = lax.broadcasted_iota(jnp.int32, (ROWS, ROWS), 1)
    same = down == across
    eye = same.astype(jnp.float32)
    moves = []
    picks = []
    for t in range(STEPS):
        dest_row = jnp.concatenate([dest[t : t + 1, :]] * 2, axis=1)
        send_row = jnp.concatenate([send[t : t + 1, :]] * 2, axis=1)
        send_col = jnp.sum(jnp.where(same, send_row, 0), axis=1, keepdims=True)
        arrives = (dest_row == down % PLANE) & (send_row == across // PLANE)
        moved = send_col == down // PLANE
        picks.append((moved & arrives) | (jnp.logical_not(moved) & same))
        moves.append(picks[t].astype(jnp.float32).astype(jnp.bfloat16))
    place2 = moves[2].astype(jnp.float32)
    place1 = dot_nn(moves[2], moves[1], None)
    place0 = dot_nn(place1.astype(jnp.bfloat16), moves[0], None)
    source = jnp.sum(jnp.where(picks[2], across, 0), axis=1, keepdims=True)
    for t in (1, 0):
        before = jnp.sum(jnp.where(picks[t], across, 0), axis=1, keepdims=True)
        before = jnp.sum(jnp.where(same, before, 0), axis=0, keepdims=True)
        source = jnp.sum(jnp.where(across == source, before, 0), axis=1, keepdims=True)
    source = jnp.sum(jnp.where(same, source, 0), axis=0, keepdims=True)
    source = jnp.minimum(jnp.maximum(source, 0), ROWS - 1)
    upper = (source >= PLANE).astype(jnp.int32)
    sidx_v[...] = jnp.zeros((8, HALF), jnp.int32)
    sidx_v[0:1, 0:ROWS] = upper
    sidx_v[1:2, 0:ROWS] = source - upper * PLANE
    to_scalar = pltpu.make_async_copy(sidx_v, sidx_s, local_sem.at[3])
    to_scalar.start()
    places = (place1, place2, eye)

    own_small.wait()
    for offset in OFFSETS:
        p = at(offset)[0]
        small_copy(p, p).wait_recv()

    def entry(e):
        return jnp.concatenate(
            [
                jnp.concatenate(
                    [buf[j * 2 + h, pl.ds(e, PLANE, stride=8), :] for j in range(2)], axis=0
                )
                for h in range(2)
            ],
            axis=1,
        )

    def entry_all(e):
        both = buf[4, pl.ds(e, PLANE, stride=8), :]
        return jnp.concatenate([both[:, : HALF // 2], both[:, HALF // 2 :]], axis=0)

    packed = entry(6)
    turned = jnp.transpose(packed)
    first = dot_nt(turned, place0)
    later = (dot_nt(turned, place1), dot_nt(turned, place2), turned)
    window = [first[CHUNK * k : CHUNK * (k + 1)] for k in range(3)]
    pick = (
        lax.broadcasted_iota(jnp.int32, (CHUNK, HALF), 0)
        == lax.broadcasted_iota(jnp.int32, (CHUNK, HALF), 1)
    ).astype(jnp.float32)
    weights = dot_nt(pick, w16[q])
    head = q // 2
    bias = dt_bias[head]
    rate = a_rate[head]
    skip = jnp.where(c == 0, d_skip[head], 0.0)
    live_cols = []
    skipped = []
    for t in range(STEPS):
        new = later[t][96 + CHUNK * t : 96 + CHUNK * (t + 1)]
        raw = later[t][192 + t : 193 + t] + bias
        live = later[t][195 + t : 196 + t]
        delta = jnp.maximum(raw, 0.0) + jnp.log1p(jnp.exp(-jnp.abs(raw)))
        decay = jnp.exp(-delta * rate)
        mixed_x = silu(
            window[0] * weights[:, 0:1]
            + window[1] * weights[:, 1:2]
            + window[2] * weights[:, 2:3]
            + new * weights[:, 3:4]
        )
        on = jnp.broadcast_to(live, (CHUNK, ROWS)) > 0.5
        dxs[t, :, 0:ROWS] = jnp.where(on, delta * mixed_x, 0.0)
        decs[t, :, 0:ROWS] = jnp.broadcast_to(
            jnp.where(live > 0.5, decay, 1.0), (8, ROWS)
        )
        skipped.append(skip * mixed_x)
        window = [
            jnp.where(on, window[1], window[0]),
            jnp.where(on, window[2], window[1]),
            jnp.where(on, new, window[2]),
        ]
        live_cols.append(column(live, same))

    window_bc = [dot_nn(place0, entry(e)) for e in range(3)]
    for copy in w_copies:
        copy.wait()
    w_bc = jnp.concatenate([wbc_v[0], wbc_v[1]], axis=1)
    window_all = [dot_nn(place0, entry_all(e)) for e in range(3)]
    for t in range(STEPS):
        new = entry(3 + t)
        if t < 2:
            new = dot_nn(places[t], new)
        both = silu(
            window_bc[0] * w_bc[0:1]
            + window_bc[1] * w_bc[1:2]
            + window_bc[2] * w_bc[2:3]
            + new * w_bc[3:4]
        )
        mixed[t, 0] = both[:, :HALF]
        mixed[t, 1] = both[:, HALF:]
        if t < 2:
            on = jnp.broadcast_to(live_cols[t], (ROWS, 2 * HALF)) > 0.5
            window_bc = [
                jnp.where(on, window_bc[1], window_bc[0]),
                jnp.where(on, window_bc[2], window_bc[1]),
                jnp.where(on, new, window_bc[2]),
            ]
        new = entry_all(3 + t)
        if t < 2:
            new = dot_nn(places[t], new)
        on = jnp.broadcast_to(live_cols[t], (ROWS, HALF // 2)) > 0.5
        window_all = [
            jnp.where(on, window_all[1], window_all[0]),
            jnp.where(on, window_all[2], window_all[1]),
            jnp.where(on, new, window_all[2]),
        ]

    def final_copy(p, part, source):
        return pltpu.make_async_remote_copy(
            src_ref=obuf.at[part, :, p], dst_ref=out_s.at[slab(source // 2, source % 2, part)],
            send_sem=o_ss.at[part, p], recv_sem=o_rs.at[part, source],
            device_id=(p, z), device_id_type=MESH,
        )

    own_finals = [
        pltpu.make_async_copy(
            obuf.at[part, :, d], out_s.at[slab(q, c, part)], local_sem.at[4 + part]
        )
        for part in range(PARTS)
    ]
    lane = lax.broadcasted_iota(jnp.int32, (PART, HALF), 1)
    lane8 = lax.broadcasted_iota(jnp.int32, (8, HALF), 1)
    zero = jnp.zeros((PART, HALF), jnp.float32)
    to_scalar.wait()
    reads = []

    def advance_part(part):
        def advance(j, dd, ys):
            f = j * PLANE + dd
            state = sbufs[part][sidx_s[0, f], sidx_s[1, f]].reshape(PART // 8, 8, HALF)
            here = lane == f
            here8 = lane8 == f
            out = []
            for t in range(STEPS):
                dx_all = dxs[t, part * PART : (part + 1) * PART, :]
                dx = jnp.sum(jnp.where(here, dx_all, 0.0), axis=1, keepdims=True)
                dec = jnp.sum(jnp.where(here8, decs[t], 0.0), axis=1, keepdims=True)
                b_row = mixed[t, 0, pl.ds(f, 1), :]
                c_row = mixed[t, 1, pl.ds(f, 1), :]
                state = state * dec[None] + (dx * b_row).reshape(PART // 8, 8, HALF)
                read = jnp.sum(state.reshape(PART, HALF) * c_row, axis=1, keepdims=True)
                out.append(jnp.where(here, read, ys[t]))
            obuf[part, j, dd] = state.reshape(PART, HALF)
            return tuple(out)

        def advance_some(i, ys):
            for k in range(2):
                for j in range(2):
                    ys = advance(j, i * 2 + k, ys)
            return ys

        return lax.fori_loop(0, PLANE // 2, advance_some, (zero,) * STEPS)

    for part in range(PARTS):
        own_states[part].wait()
        for offset in OFFSETS:
            p, qq, cc = at(offset)
            state_copy(p, qq, cc, part, p).wait_recv()
        reads.append(advance_part(part))
        if part < PARTS - 1:
            for offset in OFFSETS:
                final_copy(at(offset)[0], part, d).start()
            own_finals[part].start()

    pieces = [None] * 6
    for t in range(STEPS):
        read = jnp.concatenate([part[t][:, 0:ROWS] for part in reads], axis=0)
        read = read + skipped[t]
        back = eye if t == 2 else dot_nt(eye, places[t])
        pieces[t] = dot_nt(back, read)
        pieces[3 + t] = dot_nt(eye, window[t])
    for n in range(6):
        lo = CHUNK * (n % 4)
        flat[n // 4, :, lo : lo + CHUNK] = pieces[n]
    for n in range(3):
        lo = (HALF // 2) * ((n + 1) % 2)
        flat[1 + (n + 1) // 2, :, lo : lo + HALF // 2] = window_all[n]

    def spread_rows(dd, _):
        for j in range(2):
            for n in range(3):
                ysend[dd, j : j + 1, HALF * n : HALF * (n + 1)] = flat[
                    n, pl.ds(j * PLANE + dd, 1), :
                ]
        return 0

    lax.fori_loop(0, PLANE, spread_rows, 0)

    def read_copy(p, source):
        return pltpu.make_async_remote_copy(
            src_ref=ysend.at[p], dst_ref=yrecv.at[source],
            send_sem=y_ss.at[p], recv_sem=y_rs.at[source],
            device_id=(p, z), device_id_type=MESH,
        )

    own_read = pltpu.make_async_copy(ysend.at[d], yrecv.at[d], local_sem.at[6])
    for offset in OFFSETS:
        read_copy(at(offset)[0], d).start()
    own_read.start()
    for offset in OFFSETS:
        final_copy(at(offset)[0], PARTS - 1, d).start()
    own_finals[PARTS - 1].start()

    own_read.wait()
    for offset in OFFSETS:
        p = at(offset)[0]
        read_copy(p, p).wait_recv()
    lane2 = lax.broadcasted_iota(jnp.int32, (2, 2 * HALF), 1)
    total = jnp.zeros((2, 2 * HALF), jnp.float32)
    for qq in range(CHIPS):
        read = yrecv[2 * qq, :, 0 : 2 * HALF]
        other = yrecv[2 * qq + 1, :, 0 : 2 * HALF]
        read = read + jnp.where(lane2 < 96, other, 0.0)
        gated = read * silu(zp[qq])
        out_g[qq * 2, :, 0 : 2 * HALF] = jnp.where(lane2 < 96, gated, read)
        out_g[qq * 2 + 1, :, 0 : 2 * HALF] = other
        for cc in range(2):
            out_g[qq * 2 + cc, :, 2 * HALF :] = yrecv[qq * 2 + cc, :, 2 * HALF :]
        total = total + gated * gated
    fold = (
        lax.broadcasted_iota(jnp.int32, (2 * HALF, HALF), 0) // CHUNK
        == lax.broadcasted_iota(jnp.int32, (2 * HALF, HALF), 1)
    ).astype(jnp.float32)
    sqsend[...] = jnp.zeros((8, HALF), jnp.float32)
    sqsend[0:2, :] = dot_nn(total, fold)
    sq_copies = []
    for n, peer in enumerate(norm_peers):
        copy = pltpu.make_async_remote_copy(
            src_ref=sqsend, dst_ref=sqrecv.at[n],
            send_sem=q_ss.at[n], recv_sem=q_rs.at[n],
            device_id=peer, device_id_type=MESH,
        )
        copy.start()
        sq_copies.append(copy)
    for copy in sq_copies:
        copy.wait()
    out_tot[...] = sqsend[...] + sqrecv[0] + sqrecv[1] + sqrecv[2]

    for part in range(PARTS):
        own_finals[part].wait()
        for offset in OFFSETS:
            p = at(offset)[0]
            final_copy(p, part, p).wait_recv()
    for offset in OFFSETS:
        p, qq, cc = at(offset)
        small_copy(p, d).wait_send()
        read_copy(p, d).wait_send()
        for part in range(PARTS):
            state_copy(p, qq, cc, part, d).wait_send()
            final_copy(p, part, d).wait_send()


def local(
    ssm_state, conv_x, conv_bc, x_in, bc_in, z_in, dt_in, conv_w_x, conv_w_bc,
    dt_bias, a_rate, d_skip, norm_gain, send_slot, dest_group, active,
):
    f32 = jnp.float32
    g = lax.axis_index("tensor") // SIDE

    bc_all = jnp.concatenate([conv_bc, jnp.swapaxes(bc_in, 0, 1).astype(f32)], axis=1)
    bcx = jnp.transpose(bc_all.reshape(2, 6, PLANE, HALF // 2), (2, 1, 0, 3))
    bcx = jnp.pad(bcx.reshape(PLANE, 6, HALF), ((0, 0), (0, 2), (0, 0)))
    bc_all = lax.dynamic_index_in_dim(
        bc_all.reshape(2, 6, 2, GROUPS, 2, HALF), g, 3, keepdims=False
    )
    bcp = jnp.transpose(bc_all, (3, 0, 2, 1, 4))
    bcp = jnp.pad(bcp, ((0, 0),) * 3 + ((0, 2), (0, 0)))

    x_all = jnp.concatenate([conv_x, jnp.swapaxes(x_in, 0, 1).astype(f32)], axis=1)
    x_all = jnp.transpose(x_all.reshape(2, 6, CHIPS, CHUNK), (2, 0, 1, 3))
    dt_all = jnp.repeat(jnp.transpose(dt_in.astype(f32), (2, 1, 0)), 2, axis=0)
    live = jnp.broadcast_to(jnp.transpose(active).astype(f32)[None], (CHIPS, 2, STEPS))
    xp = jnp.concatenate(
        [x_all.reshape(CHIPS, 2, 192), dt_all, live, jnp.zeros((CHIPS, 2, 58), f32)],
        axis=2,
    )
    zp = jnp.transpose(z_in.astype(f32).reshape(STEPS, 2, CHIPS, CHUNK), (2, 1, 0, 3))
    zp = jnp.pad(zp.reshape(CHIPS, 2, 96), ((0, 0), (0, 0), (0, 160)))
    w16 = jnp.transpose(conv_w_x.reshape(4, CHIPS, CHUNK), (1, 0, 2))
    w16 = jnp.pad(w16, ((0, 0), (0, 4), (0, HALF - CHUNK)))

    vmem = pl.BlockSpec(memory_space=pltpu.VMEM)
    smem = pl.BlockSpec(memory_space=pltpu.SMEM)
    hbm = pl.BlockSpec(memory_space=pl.ANY)
    dma = pltpu.SemaphoreType.DMA
    out_s, out_g, out_tot = pl.pallas_call(
        kernel,
        out_shape=(
            jax.ShapeDtypeStruct((2, 512, 256), f32),
            jax.ShapeDtypeStruct((PLANE, 2, 384), f32),
            jax.ShapeDtypeStruct((8, HALF), f32),
        ),
        in_specs=[hbm] + [vmem] * 7 + [hbm] + [smem] * 3,
        out_specs=(hbm, vmem, vmem),
        scratch_shapes=[
            pltpu.VMEM((PLANE, 5, 8, HALF), f32),
            pltpu.VMEM((5, PLANE * 8, HALF), f32),
            pltpu.VMEM((2, PLANE, PART, HALF), f32),
            pltpu.VMEM((2, PLANE, PART, HALF), f32),
            pltpu.VMEM((PARTS, 2, PLANE, PART, HALF), f32),
            pltpu.VMEM((STEPS, CHUNK, HALF), f32),
            pltpu.VMEM((STEPS, 8, HALF), f32),
            pltpu.VMEM((STEPS, 2, ROWS, HALF), f32),
            pltpu.VMEM((3, ROWS, HALF), f32),
            pltpu.VMEM((PLANE, 2, 384), f32),
            pltpu.VMEM((PLANE, 2, 384), f32),
            pltpu.VMEM((8, HALF), f32),
            pltpu.VMEM((3, 8, HALF), f32),
            pltpu.VMEM((8, HALF), jnp.int32),
            pltpu.VMEM((2, 4, HALF), f32),
            pltpu.SMEM((8, HALF), jnp.int32),
            dma((2,)),
            dma((PLANE,)), dma((PLANE,)),
            dma((PARTS, PLANE)), dma((PARTS, PLANE)),
            dma((PARTS, PLANE)), dma((PARTS, PLANE)),
            dma((PLANE,)), dma((PLANE,)),
            dma((4,)), dma((4,)),
            dma((8,)),
        ],
        compiler_params=pltpu.CompilerParams(
            collective_id=0, has_side_effects=True, vmem_limit_bytes=48 * 2**20
        ),
    )(
        ssm_state.reshape(2, 512, 256), bcp, bcx, xp, zp, dest_group, send_slot, w16,
        conv_w_bc, dt_bias, a_rate, d_skip,
    )

    factor = lax.rsqrt(out_tot[0:2, 0:STEPS] / NORM_WIDTH + 1e-05)
    packed = out_g.reshape(CHIPS, 2, 2, 384)[:, 0, :, 0:192].reshape(CHIPS, 2, 6, CHUNK)
    normed = (
        packed[:, :, 0:3] * factor[None, :, :, None]
        * norm_gain.reshape(CHIPS, 1, 1, CHUNK)
    )
    normed = jnp.where(jnp.transpose(active)[None, :, :, None] > 0, normed, 0.0)
    mixer = jnp.transpose(normed.astype(jnp.bfloat16), (2, 1, 0, 3)).reshape(STEPS, 2, 512)
    final_x = jnp.transpose(packed[:, :, 3:6], (1, 2, 0, 3)).reshape(2, 3, 512)
    final_bc = out_g[:, :, 192:].reshape(PLANE, 2, 3, HALF // 2)
    final_bc = jnp.transpose(final_bc, (1, 2, 0, 3)).reshape(2, 3, 2048)
    return mixer, out_s.reshape(ssm_state.shape), final_x, final_bc


def solution(mesh):
    return jax.shard_map(
        local,
        mesh=mesh,
        in_specs=(
            P("dp", "tensor", None, None),
            P("dp", None, "tensor"),
            P("dp", None, None),
            P(None, "dp", "tensor"),
            P(None, "dp", None),
            P(None, "dp", "tensor"),
            P(None, "dp", "tensor"),
            P(None, "tensor"),
            P(),
            P("tensor"),
            P("tensor"),
            P("tensor"),
            P("tensor"),
            P(),
            P(),
            P(None, "dp"),
        ),
        out_specs=(
            P(None, "dp", "tensor"),
            P("dp", "tensor", None, None),
            P("dp", None, "tensor"),
            P("dp", None, None),
        ),
        check_vma=False,
    )
```

```python
import jax
import jax.numpy as jnp
from jax import lax
from jax.experimental import pallas as pl
from jax.experimental.pallas import tpu as pltpu
from jax.sharding import PartitionSpec as P

MESH = pl.DeviceIdType.MESH
HIGH = lax.Precision.HIGHEST
STEPS = 3
SIDE = 4
CHIPS = 16
PLANE = 32
ROWS = 64
CHUNK = 32
FIXED = 15
VMEM_BYTES = 63 * 2**20
PARTS = 2
PART = CHUNK // PARTS
HALF = 128
TENSOR = 16
GROUPS = 4
NORM_WIDTH = 2048

HOPS = (
    (2, 2), (2, 1), (1, 2), (2, 3), (3, 2), (2, 0), (0, 2), (1, 1),
    (3, 3), (1, 3), (3, 1), (1, 0), (0, 1), (3, 0), (0, 3), (0, 0),
)
OFFSETS = tuple(
    (kc, kx, ky) for kx, ky in HOPS for kc in (0, 1) if (kc, kx, ky) != (0, 0, 0)
)


def dot_nt(a, b, precision=HIGH):
    return lax.dot_general(
        a, b, (((1,), (1,)), ((), ())), precision=precision,
        preferred_element_type=jnp.float32,
    )


def dot_nn(a, b, precision=HIGH):
    return lax.dot_general(
        a, b, (((1,), (0,)), ((), ())), precision=precision,
        preferred_element_type=jnp.float32,
    )


def stack4(v):
    return jnp.concatenate([v[:, HALF * a : HALF * (a + 1)] for a in range(4)], axis=0)


def silu(v):
    return v / (1.0 + jnp.exp(-v))


def column(row_values, same):
    return jnp.sum(jnp.where(same, row_values, 0.0), axis=1, keepdims=True)


def kernel(
    ssm, *refs,
):
    given, refs = refs[:FIXED], refs[FIXED:]
    outs, held, refs = refs[:4], refs[4 : 4 + FIXED], refs[4 + FIXED :]
    run(ssm, *held, *outs, given, held, *refs)


def run(
    ssm, cx, xin, cbc, bcin, zin, dtin, wx, wbc, gain, dest, send,
    active, dt_bias, a_rate, d_skip,
    out_s, out_m, out_x, out_bc, given, held, in_sem,
    pk, buf, sbuf0, sbuf1, obuf, dxs, decs, mixed, flat, ysend, yrecv,
    sqsend, sqrecv, sidx_v, bcf, model, extra, sidx_s,
    pk_ss, pk_rs, s_ss, s_rs, o_ss, o_rs, y_ss, y_rs, q_ss, q_rs, local_sem,
):
    sbufs = (sbuf0, sbuf1)
    d = lax.axis_index("dp")
    z = lax.axis_index("tensor")
    c = d % 2
    q = d // 2
    x = q % SIDE
    y = q // SIDE
    g = z // SIDE
    m = z % SIDE

    def at(offset):
        kc, kx, ky = offset
        cc = (c + kc) % 2
        qq = ((y + ky) % SIDE) * SIDE + (x + kx) % SIDE
        return qq * 2 + cc, qq, cc

    norm_peers = [(d, g * SIDE + (m + i) % SIDE) for i in range(1, SIDE)]

    loads = [
        pltpu.make_async_copy(source, target, in_sem.at[n])
        for n, (source, target) in enumerate(zip(given, held))
    ]
    for copy in loads:
        copy.start()
    barrier = pltpu.get_barrier_semaphore()
    signals = 0
    for offset in OFFSETS:
        pl.semaphore_signal(barrier, inc=1, device_id=(at(offset)[0], z), device_id_type=MESH)
        signals += 1
    for peer in norm_peers:
        pl.semaphore_signal(barrier, inc=1, device_id=peer, device_id_type=MESH)
        signals += 1

    for copy in loads:
        copy.wait()
    lane8 = lax.broadcasted_iota(jnp.int32, (8, HALF), 1)
    lane1 = lax.broadcasted_iota(jnp.int32, (1, HALF), 1)
    for t in range(STEPS):
        bcf[t] = bcin[t].astype(jnp.float32)
    extra[...] = jnp.zeros((8, HALF), jnp.float32)
    for t in range(STEPS):
        extra[0:2, 8 * t : 8 * t + 8] = dtin[t].astype(jnp.float32)
    for j in range(2):
        for t in range(STEPS):
            extra[j : j + 1, :] = jnp.where(
                lane1 == 24 + t, active[j, t].astype(jnp.float32), extra[j : j + 1, :]
            )
    model[...] = jnp.zeros((2, 4, 8, HALF), jnp.float32)
    for cc in range(2):
        for h in range(2):
            base = pl.multiple_of(h * 1024 + g * 2 * HALF + cc * HALF, HALF)
            for j in range(2):
                for e in range(6):
                    table = cbc if e < 3 else bcf
                    model[cc, 2 * j + h, e : e + 1, :] = table[
                        e % 3, j : j + 1, pl.ds(base, HALF)
                    ]
        for j in range(2):
            model[cc, 2 * j, 7:8, :] = extra[j : j + 1, :]

    def fill(qq, _):
        place = pl.ds(pl.multiple_of(qq * HALF, HALF), HALF)
        for cc in range(2):
            pk[qq * 2 + cc, 0:4] = model[cc]
            pk[qq * 2 + cc, 4] = jnp.zeros((8, HALF), jnp.float32)
        for e in range(6):
            table = cbc if e < 3 else bcf
            both = table[e % 3, :, place]
            turn = pltpu.roll(both, HALF // 2, 1)
            low = lane1 < HALF // 2
            pk[qq * 2, 4, e : e + 1, :] = jnp.where(low, both[0:1], turn[1:2])
            pk[qq * 2 + 1, 4, e : e + 1, :] = jnp.where(low, turn[0:1], both[1:2])
        return 0

    lax.fori_loop(0, CHIPS, fill, 0)
    stacks = [stack4(cx[e]) for e in range(3)]
    stacks += [stack4(xin[e].astype(jnp.float32)) for e in range(3)]
    for b in range(4):
        for h in range(2):
            row = jnp.zeros((8, HALF), jnp.float32)
            for e in range(4 * h, min(6, 4 * h + 4)):
                moved = pltpu.roll(stacks[e], (CHUNK * (e % 4 - b)) % HALF, 1)
                row = jnp.where(lane8 // CHUNK == e % 4, moved, row)
            for a in range(4):
                for j in range(2):
                    for cc in range(2):
                        p = 2 * (4 * a + b) + cc
                        pk[p, 2 * j + h, 6:7, :] = row[2 * a + j : 2 * a + j + 1]

    pl.semaphore_wait(barrier, signals)

    def lines(device):
        return pl.ds(pl.multiple_of(device * 8, 8), 8)

    def small_copy(p, source):
        return pltpu.make_async_remote_copy(
            src_ref=pk.at[p], dst_ref=buf.at[:, lines(source)],
            send_sem=pk_ss.at[p], recv_sem=pk_rs.at[source],
            device_id=(p, z), device_id_type=MESH,
        )

    def slab(qq, cc, part):
        return (
            slice(None),
            pl.ds(pl.multiple_of(qq * CHUNK + part * PART, PART), PART),
            pl.ds(pl.multiple_of(cc * HALF, HALF), HALF),
        )

    def state_copy(p, qq, cc, part, source):
        return pltpu.make_async_remote_copy(
            src_ref=ssm.at[slab(qq, cc, part)],
            dst_ref=sbufs[part].at[:, source],
            send_sem=s_ss.at[part, p], recv_sem=s_rs.at[part, source],
            device_id=(p, z), device_id_type=MESH,
        )

    own_small = pltpu.make_async_copy(pk.at[d], buf.at[:, lines(d)], local_sem.at[0])
    own_states = [
        pltpu.make_async_copy(
            ssm.at[slab(q, c, part)], sbufs[part].at[:, d], local_sem.at[1 + part]
        )
        for part in range(PARTS)
    ]
    for offset in OFFSETS:
        small_copy(at(offset)[0], d).start()
    own_small.start()
    for part in range(PARTS):
        for offset in OFFSETS:
            p, qq, cc = at(offset)
            state_copy(p, qq, cc, part, d).start()
        own_states[part].start()

    down = lax.broadcasted_iota(jnp.int32, (ROWS, ROWS), 0)
    across = lax.broadcasted_iota(jnp.int32, (ROWS, ROWS), 1)
    same = down == across
    eye = same.astype(jnp.float32)
    moves = []
    picks = []
    for t in range(STEPS):
        dest_row = jnp.concatenate([dest[t : t + 1, :]] * 2, axis=1)
        send_row = jnp.concatenate([send[t : t + 1, :]] * 2, axis=1)
        send_col = jnp.sum(jnp.where(same, send_row, 0), axis=1, keepdims=True)
        arrives = (dest_row == down % PLANE) & (send_row == across // PLANE)
        moved = send_col == down // PLANE
        picks.append((moved & arrives) | (jnp.logical_not(moved) & same))
        moves.append(picks[t].astype(jnp.float32).astype(jnp.bfloat16))
    place2 = moves[2].astype(jnp.float32)
    place1 = dot_nn(moves[2], moves[1], None)
    place0 = dot_nn(place1.astype(jnp.bfloat16), moves[0], None)
    source = jnp.sum(jnp.where(picks[2], across, 0), axis=1, keepdims=True)
    for t in (1, 0):
        before = jnp.sum(jnp.where(picks[t], across, 0), axis=1, keepdims=True)
        before = jnp.sum(jnp.where(same, before, 0), axis=0, keepdims=True)
        source = jnp.sum(jnp.where(across == source, before, 0), axis=1, keepdims=True)
    source = jnp.sum(jnp.where(same, source, 0), axis=0, keepdims=True)
    source = jnp.minimum(jnp.maximum(source, 0), ROWS - 1)
    upper = (source >= PLANE).astype(jnp.int32)
    sidx_v[...] = jnp.zeros((8, HALF), jnp.int32)
    sidx_v[0:1, 0:ROWS] = upper
    sidx_v[1:2, 0:ROWS] = source - upper * PLANE
    to_scalar = pltpu.make_async_copy(sidx_v, sidx_s, local_sem.at[3])
    to_scalar.start()
    places = (place1, place2, eye)

    own_small.wait()
    for offset in OFFSETS:
        p = at(offset)[0]
        small_copy(p, p).wait_recv()

    def entry(e):
        return jnp.concatenate(
            [
                jnp.concatenate(
                    [buf[j * 2 + h, pl.ds(e, PLANE, stride=8), :] for j in range(2)], axis=0
                )
                for h in range(2)
            ],
            axis=1,
        )

    def entry_all(e):
        both = buf[4, pl.ds(e, PLANE, stride=8), :]
        return jnp.concatenate([both[:, : HALF // 2], both[:, HALF // 2 :]], axis=0)

    packed = entry(6)
    marks = jnp.concatenate(
        [buf[j * 2, pl.ds(7, PLANE, stride=8), :] for j in range(2)], axis=0
    )
    turned = jnp.transpose(packed)
    marks = jnp.transpose(marks)[0:CHUNK]
    first = dot_nt(turned[0:96], place0)
    fresh_x = []
    fresh_marks = []
    for t in range(STEPS):
        new = turned[96 + CHUNK * t : 96 + CHUNK * (t + 1)]
        fresh_x.append(new if t == 2 else dot_nt(new, places[t]))
        fresh_marks.append(marks if t == 2 else dot_nt(marks, places[t]))
    window = [first[CHUNK * k : CHUNK * (k + 1)] for k in range(3)]
    pick = (
        lax.broadcasted_iota(jnp.int32, (CHUNK, HALF), 0) + CHUNK * (q % 4)
        == lax.broadcasted_iota(jnp.int32, (CHUNK, HALF), 1)
    ).astype(jnp.float32)
    quarter = wx[:, pl.ds(pl.multiple_of(q // 4 * HALF, HALF), HALF)]
    weights = dot_nt(
        pick, jnp.concatenate([quarter, jnp.zeros((4, HALF), jnp.float32)], axis=0)
    )
    of_head = lax.broadcasted_iota(jnp.int32, (8, ROWS), 0) == q // 2
    head = q // 2
    bias = dt_bias[head]
    rate = a_rate[head]
    skip = jnp.where(c == 0, d_skip[head], 0.0)
    live_cols = []
    skipped = []
    for t in range(STEPS):
        new = fresh_x[t]
        raw = jnp.where(of_head, fresh_marks[t][8 * t : 8 * t + 8], 0.0)
        raw = jnp.sum(raw, axis=0, keepdims=True) + bias
        live = fresh_marks[t][24 + t : 25 + t]
        delta = jnp.maximum(raw, 0.0) + jnp.log1p(jnp.exp(-jnp.abs(raw)))
        decay = jnp.exp(-delta * rate)
        mixed_x = silu(
            window[0] * weights[:, 0:1]
            + window[1] * weights[:, 1:2]
            + window[2] * weights[:, 2:3]
            + new * weights[:, 3:4]
        )
        on = jnp.broadcast_to(live, (CHUNK, ROWS)) > 0.5
        dxs[t, :, 0:ROWS] = jnp.where(on, delta * mixed_x, 0.0)
        decs[t, :, 0:ROWS] = jnp.broadcast_to(
            jnp.where(live > 0.5, decay, 1.0), (8, ROWS)
        )
        skipped.append(skip * mixed_x)
        window = [
            jnp.where(on, window[1], window[0]),
            jnp.where(on, window[2], window[1]),
            jnp.where(on, new, window[2]),
        ]
        live_cols.append(column(live, same))

    window_bc = [dot_nn(place0, entry(e)) for e in range(3)]
    w_bc = jnp.concatenate(
        [
            wbc[:, pl.ds(pl.multiple_of(h * 1024 + g * 2 * HALF + c * HALF, HALF), HALF)]
            for h in range(2)
        ],
        axis=1,
    )
    window_all = [dot_nn(place0, entry_all(e)) for e in range(3)]
    for t in range(STEPS):
        new = entry(3 + t)
        if t < 2:
            new = dot_nn(places[t], new)
        both = silu(
            window_bc[0] * w_bc[0:1]
            + window_bc[1] * w_bc[1:2]
            + window_bc[2] * w_bc[2:3]
            + new * w_bc[3:4]
        )
        mixed[t, 0] = both[:, :HALF]
        mixed[t, 1] = both[:, HALF:]
        if t < 2:
            on = jnp.broadcast_to(live_cols[t], (ROWS, 2 * HALF)) > 0.5
            window_bc = [
                jnp.where(on, window_bc[1], window_bc[0]),
                jnp.where(on, window_bc[2], window_bc[1]),
                jnp.where(on, new, window_bc[2]),
            ]
        new = entry_all(3 + t)
        if t < 2:
            new = dot_nn(places[t], new)
        on = jnp.broadcast_to(live_cols[t], (ROWS, HALF // 2)) > 0.5
        window_all = [
            jnp.where(on, window_all[1], window_all[0]),
            jnp.where(on, window_all[2], window_all[1]),
            jnp.where(on, new, window_all[2]),
        ]

    def final_copy(p, part, source):
        return pltpu.make_async_remote_copy(
            src_ref=obuf.at[part, :, p], dst_ref=out_s.at[slab(source // 2, source % 2, part)],
            send_sem=o_ss.at[part, p], recv_sem=o_rs.at[part, source],
            device_id=(p, z), device_id_type=MESH,
        )

    own_finals = [
        pltpu.make_async_copy(
            obuf.at[part, :, d], out_s.at[slab(q, c, part)], local_sem.at[4 + part]
        )
        for part in range(PARTS)
    ]
    lane = lax.broadcasted_iota(jnp.int32, (PART, HALF), 1)
    zero = jnp.zeros((PART, HALF), jnp.float32)
    to_scalar.wait()
    reads = []

    def advance_part(part):
        def advance(j, dd, ys):
            f = j * PLANE + dd
            state = sbufs[part][sidx_s[0, f], sidx_s[1, f]].reshape(PART // 8, 8, HALF)
            here = lane == f
            here8 = lane8 == f
            out = []
            for t in range(STEPS):
                dx_all = dxs[t, part * PART : (part + 1) * PART, :]
                dx = jnp.sum(jnp.where(here, dx_all, 0.0), axis=1, keepdims=True)
                dec = jnp.sum(jnp.where(here8, decs[t], 0.0), axis=1, keepdims=True)
                b_row = mixed[t, 0, pl.ds(f, 1), :]
                c_row = mixed[t, 1, pl.ds(f, 1), :]
                state = state * dec[None] + (dx * b_row).reshape(PART // 8, 8, HALF)
                read = jnp.sum(state.reshape(PART, HALF) * c_row, axis=1, keepdims=True)
                out.append(jnp.where(here, read, ys[t]))
            obuf[part, j, dd] = state.reshape(PART, HALF)
            return tuple(out)

        def advance_some(i, ys):
            for k in range(2):
                for j in range(2):
                    ys = advance(j, i * 2 + k, ys)
            return ys

        return lax.fori_loop(0, PLANE // 2, advance_some, (zero,) * STEPS)

    for part in range(PARTS):
        own_states[part].wait()
        for offset in OFFSETS:
            p, qq, cc = at(offset)
            state_copy(p, qq, cc, part, p).wait_recv()
        reads.append(advance_part(part))
        if part < PARTS - 1:
            for offset in OFFSETS:
                final_copy(at(offset)[0], part, d).start()
            own_finals[part].start()

    pieces = [None] * 6
    for t in range(STEPS):
        read = jnp.concatenate([part[t][:, 0:ROWS] for part in reads], axis=0)
        read = read + skipped[t]
        back = eye if t == 2 else dot_nt(eye, places[t])
        pieces[t] = dot_nt(back, read)
        pieces[3 + t] = dot_nt(eye, window[t])
    for n in range(6):
        lo = CHUNK * (n % 4)
        flat[n // 4, :, lo : lo + CHUNK] = pieces[n]
    for n in range(3):
        lo = (HALF // 2) * ((n + 1) % 2)
        flat[1 + (n + 1) // 2, :, lo : lo + HALF // 2] = window_all[n]

    def spread_rows(dd, _):
        for j in range(2):
            for n in range(3):
                ysend[dd, j : j + 1, HALF * n : HALF * (n + 1)] = flat[
                    n, pl.ds(j * PLANE + dd, 1), :
                ]
        return 0

    lax.fori_loop(0, PLANE, spread_rows, 0)

    def read_copy(p, source):
        return pltpu.make_async_remote_copy(
            src_ref=ysend.at[p], dst_ref=yrecv.at[source],
            send_sem=y_ss.at[p], recv_sem=y_rs.at[source],
            device_id=(p, z), device_id_type=MESH,
        )

    own_read = pltpu.make_async_copy(ysend.at[d], yrecv.at[d], local_sem.at[6])
    for offset in OFFSETS:
        read_copy(at(offset)[0], d).start()
    own_read.start()
    for offset in OFFSETS:
        final_copy(at(offset)[0], PARTS - 1, d).start()
    own_finals[PARTS - 1].start()

    own_read.wait()
    for offset in OFFSETS:
        p = at(offset)[0]
        read_copy(p, p).wait_recv()

    def gather4(h, b, cc):
        return jnp.concatenate(
            [
                yrecv[2 * (4 * a + b) + cc, :, HALF * h : HALF * (h + 1)]
                for a in range(4)
            ],
            axis=0,
        )

    wide = [jnp.zeros((8, HALF), jnp.float32)] * 6
    for b in range(4):
        tiles = [gather4(0, b, 0), gather4(1, b, 0)]
        summed = tiles[0] + gather4(0, b, 1)
        for e in range(6):
            tile = summed if e < 3 else tiles[e // 4]
            moved = pltpu.roll(tile, (CHUNK * (b - e % 4)) % HALF, 1)
            wide[e] = jnp.where(lane8 // CHUNK == b, moved, wide[e])
    gated = []
    squares = jnp.zeros((8, HALF), jnp.float32)
    for t in range(STEPS):
        gated.append(wide[t] * silu(stack4(zin[t].astype(jnp.float32))))
        part = jnp.sum(gated[t] * gated[t], axis=1, keepdims=True)
        squares = jnp.where(lane8 == t, part, squares)
    sqsend[...] = squares
    sq_copies = []
    for n, peer in enumerate(norm_peers):
        copy = pltpu.make_async_remote_copy(
            src_ref=sqsend, dst_ref=sqrecv.at[n],
            send_sem=q_ss.at[n], recv_sem=q_rs.at[n],
            device_id=peer, device_id_type=MESH,
        )
        copy.start()
        sq_copies.append(copy)
    low = lane8[0:2] < HALF // 2
    for a in range(4):
        for e in range(3):
            out_x[e, :, HALF * a : HALF * (a + 1)] = wide[3 + e][2 * a : 2 * a + 2]
    for qq in range(CHIPS):
        for e in range(3):
            tile = HALF * (1 + (e + 1) // 2)
            left = yrecv[2 * qq, :, tile : tile + HALF]
            right = yrecv[2 * qq + 1, :, tile : tile + HALF]
            if e == 1:
                right = pltpu.roll(right, HALF // 2, 1)
            else:
                left = pltpu.roll(left, HALF // 2, 1)
            out_bc[e, :, HALF * qq : HALF * (qq + 1)] = jnp.where(low, left, right)
    for copy in sq_copies:
        copy.wait()
    total = sqsend[...] + sqrecv[0] + sqrecv[1] + sqrecv[2]
    even = lax.broadcasted_iota(jnp.int32, (8, HALF), 0) % 2 == 0
    gains = jnp.concatenate([gain[n // 2 : n // 2 + 1, :] for n in range(8)], axis=0)
    for t in range(STEPS):
        col = jnp.sum(jnp.where(lane8 == t, total, 0.0), axis=1, keepdims=True)
        col = jnp.broadcast_to(col, (8, HALF))
        of_even = jnp.sum(jnp.where(even, col, 0.0), axis=0, keepdims=True)
        of_odd = jnp.sum(jnp.where(even, 0.0, col), axis=0, keepdims=True)
        factor = lax.rsqrt(jnp.where(even, of_even, of_odd) / NORM_WIDTH + 1e-05)
        on = jnp.where(even, active[0, t], active[1, t]) > 0
        normed = jnp.where(on, gated[t] * factor * gains, 0.0)
        for a in range(4):
            out_m[t, :, HALF * a : HALF * (a + 1)] = normed[2 * a : 2 * a + 2]

    for part in range(PARTS):
        own_finals[part].wait()
        for offset in OFFSETS:
            p = at(offset)[0]
            final_copy(p, part, p).wait_recv()
    for offset in OFFSETS:
        p, qq, cc = at(offset)
        small_copy(p, d).wait_send()
        read_copy(p, d).wait_send()
        for part in range(PARTS):
            state_copy(p, qq, cc, part, d).wait_send()
            final_copy(p, part, d).wait_send()


def finish(*refs):
    given, outs, held, mixer, sems = refs[:4], refs[4:8], refs[8:12], refs[12], refs[13]
    loads = [
        pltpu.make_async_copy(source, target, sems.at[0, n])
        for n, (source, target) in enumerate(zip(given, held))
    ]
    for copy in loads:
        copy.start()
    stores = [
        pltpu.make_async_copy(source, target, sems.at[1, n])
        for n, (source, target) in enumerate(zip((*held[:3], mixer), outs))
    ]
    for n in (1, 2):
        loads[n].wait()
        stores[n].start()
    loads[3].wait()
    mixer[...] = held[3][...].astype(jnp.bfloat16)
    stores[3].start()
    loads[0].wait()
    stores[0].start()
    for copy in stores:
        copy.wait()


def local(
    ssm_state, conv_x, conv_bc, x_in, bc_in, z_in, dt_in, conv_w_x, conv_w_bc,
    dt_bias, a_rate, d_skip, norm_gain, send_slot, dest_group, active,
):
    f32 = jnp.float32
    vmem = pl.BlockSpec(memory_space=pltpu.VMEM)
    hbm = pl.BlockSpec(memory_space=pltpu.HBM)
    dma = pltpu.SemaphoreType.DMA
    shapes = [
        jax.ShapeDtypeStruct((2, 512, 256), f32),
        jax.ShapeDtypeStruct((STEPS, 2, 512), f32),
        jax.ShapeDtypeStruct((3, 2, 512), f32),
        jax.ShapeDtypeStruct((3, 2, 2048), f32),
    ]
    state, mix, final_x, final_bc = pl.pallas_call(
        kernel,
        out_shape=tuple(shapes),
        in_specs=[hbm] * (1 + FIXED),
        out_specs=(hbm, vmem, vmem, vmem),
        scratch_shapes=[
            pltpu.VMEM((3, 2, 512), f32),
            pltpu.VMEM((STEPS, 2, 512), jnp.bfloat16),
            pltpu.VMEM((3, 2, 2048), f32),
            pltpu.VMEM((STEPS, 2, 2048), jnp.bfloat16),
            pltpu.VMEM((STEPS, 2, 512), jnp.bfloat16),
            pltpu.VMEM((STEPS, 2, 8), jnp.bfloat16),
            pltpu.VMEM((4, 512), f32),
            pltpu.VMEM((4, 2048), f32),
            pltpu.VMEM((4, HALF), f32),
            pltpu.VMEM((STEPS, PLANE), jnp.int32),
            pltpu.VMEM((STEPS, PLANE), jnp.int32),
            pltpu.SMEM((2, STEPS), jnp.int32),
            pltpu.SMEM((8,), f32),
            pltpu.SMEM((8,), f32),
            pltpu.SMEM((8,), f32),
            dma((16,)),
            pltpu.VMEM((PLANE, 5, 8, HALF), f32),
            pltpu.VMEM((5, PLANE * 8, HALF), f32),
            pltpu.VMEM((2, PLANE, PART, HALF), f32),
            pltpu.VMEM((2, PLANE, PART, HALF), f32),
            pltpu.VMEM((PARTS, 2, PLANE, PART, HALF), f32),
            pltpu.VMEM((STEPS, CHUNK, HALF), f32),
            pltpu.VMEM((STEPS, 8, HALF), f32),
            pltpu.VMEM((STEPS, 2, ROWS, HALF), f32),
            pltpu.VMEM((3, ROWS, HALF), f32),
            pltpu.VMEM((PLANE, 2, 384), f32),
            pltpu.VMEM((PLANE, 2, 384), f32),
            pltpu.VMEM((8, HALF), f32),
            pltpu.VMEM((3, 8, HALF), f32),
            pltpu.VMEM((8, HALF), jnp.int32),
            pltpu.VMEM((STEPS, 2, 2048), f32),
            pltpu.VMEM((2, 4, 8, HALF), f32),
            pltpu.VMEM((8, HALF), f32),
            pltpu.SMEM((8, HALF), jnp.int32),
            dma((PLANE,)), dma((PLANE,)),
            dma((PARTS, PLANE)), dma((PARTS, PLANE)),
            dma((PARTS, PLANE)), dma((PARTS, PLANE)),
            dma((PLANE,)), dma((PLANE,)),
            dma((4,)), dma((4,)),
            dma((8,)),
        ],
        compiler_params=pltpu.CompilerParams(
            collective_id=0, has_side_effects=True, vmem_limit_bytes=VMEM_BYTES
        ),
    )(
        ssm_state.reshape(2, 512, 256), jnp.swapaxes(conv_x, 0, 1), x_in,
        jnp.swapaxes(conv_bc, 0, 1), bc_in, z_in, dt_in, conv_w_x, conv_w_bc,
        norm_gain.reshape(4, HALF), dest_group, send_slot, jnp.transpose(active),
        dt_bias, a_rate, d_skip,
    )
    bits = jax.ShapeDtypeStruct((STEPS, 2, 512), jnp.bfloat16)
    state, final_x, final_bc, mixer = pl.pallas_call(
        finish,
        out_shape=(shapes[0], shapes[2], shapes[3], bits),
        in_specs=[hbm] * 4,
        out_specs=(hbm,) * 4,
        scratch_shapes=[
            pltpu.VMEM(shapes[n].shape, f32) for n in (0, 2, 3, 1)
        ] + [pltpu.VMEM(bits.shape, jnp.bfloat16), dma((2, 4))],
        compiler_params=pltpu.CompilerParams(vmem_limit_bytes=VMEM_BYTES),
    )(state, final_x, final_bc, mix)
    return (
        mixer,
        state.reshape(ssm_state.shape),
        jnp.swapaxes(final_x, 0, 1),
        jnp.swapaxes(final_bc, 0, 1),
    )


def solution(mesh):
    return jax.shard_map(
        local,
        mesh=mesh,
        in_specs=(
            P("dp", "tensor", None, None),
            P("dp", None, "tensor"),
            P("dp", None, None),
            P(None, "dp", "tensor"),
            P(None, "dp", None),
            P(None, "dp", "tensor"),
            P(None, "dp", "tensor"),
            P(None, "tensor"),
            P(),
            P("tensor"),
            P("tensor"),
            P("tensor"),
            P("tensor"),
            P(),
            P(),
            P(None, "dp"),
        ),
        out_specs=(
            P(None, "dp", "tensor"),
            P("dp", "tensor", None, None),
            P("dp", None, "tensor"),
            P("dp", None, None),
        ),
        check_vma=False,
    )
```

```python
import jax
import jax.numpy as jnp
from jax import lax
from jax.experimental import pallas as pl
from jax.experimental.pallas import tpu as pltpu
from jax.sharding import PartitionSpec as P

MESH = pl.DeviceIdType.MESH
HIGH = lax.Precision.HIGHEST
STEPS = 3
SIDE = 4
CHIPS = 16
PLANE = 32
ROWS = 64
CHUNK = 32
FIXED = 15
FEW = 16
VMEM_BYTES = 63 * 2**20
PARTS = 2
PART = CHUNK // PARTS
HALF = 128
TENSOR = 16
GROUPS = 4
NORM_WIDTH = 2048

HOPS = (
    (2, 2), (2, 1), (1, 2), (2, 3), (3, 2), (2, 0), (0, 2), (1, 1),
    (3, 3), (1, 3), (3, 1), (1, 0), (0, 1), (3, 0), (0, 3), (0, 0),
)
OFFSETS = tuple(
    (kc, kx, ky) for kx, ky in HOPS for kc in (0, 1) if (kc, kx, ky) != (0, 0, 0)
)


def dot_nt(a, b, precision=HIGH):
    return lax.dot_general(
        a, b, (((1,), (1,)), ((), ())), precision=precision,
        preferred_element_type=jnp.float32,
    )


def dot_nn(a, b, precision=HIGH):
    return lax.dot_general(
        a, b, (((1,), (0,)), ((), ())), precision=precision,
        preferred_element_type=jnp.float32,
    )


def stack4(v):
    return jnp.concatenate([v[:, HALF * a : HALF * (a + 1)] for a in range(4)], axis=0)


def silu(v):
    return v / (1.0 + jnp.exp(-v))


def column(row_values, same):
    return jnp.sum(jnp.where(same, row_values, 0.0), axis=1, keepdims=True)


def kernel(
    ssm, *refs,
):
    given, refs = refs[:FIXED], refs[FIXED:]
    outs, held, refs = refs[:4], refs[4 : 4 + FIXED], refs[4 + FIXED :]
    run(ssm, *held, *outs, given, held, *refs)


def run(
    ssm, cx, xin, cbc, bcin, zin, dtin, wx, wbc, gain, dest, send,
    active, dt_bias, a_rate, d_skip,
    out_s, out_m, out_x, out_bc, given, held, in_sem,
    pk, buf, sbuf0, sbuf1, obuf, dxs, decs, mixed, flat, ysend, yrecv, ends, pushes, fades,
    sqsend, sqrecv, sidx_v, bcf, model, extra, sidx_s,
    pk_ss, pk_rs, s_ss, s_rs, o_ss, o_rs, y_ss, y_rs, q_ss, q_rs, local_sem,
):
    sbufs = (sbuf0, sbuf1)
    d = lax.axis_index("dp")
    z = lax.axis_index("tensor")
    c = d % 2
    q = d // 2
    x = q % SIDE
    y = q // SIDE
    g = z // SIDE
    m = z % SIDE

    def at(offset):
        kc, kx, ky = offset
        cc = (c + kc) % 2
        qq = ((y + ky) % SIDE) * SIDE + (x + kx) % SIDE
        return qq * 2 + cc, qq, cc

    norm_peers = [(d, g * SIDE + (m + i) % SIDE) for i in range(1, SIDE)]

    loads = [
        pltpu.make_async_copy(source, target, in_sem.at[n])
        for n, (source, target) in enumerate(zip(given, held))
    ]
    for copy in loads:
        copy.start()
    barrier = pltpu.get_barrier_semaphore()
    signals = 0
    for offset in OFFSETS:
        pl.semaphore_signal(barrier, inc=1, device_id=(at(offset)[0], z), device_id_type=MESH)
        signals += 1
    for peer in norm_peers:
        pl.semaphore_signal(barrier, inc=1, device_id=peer, device_id_type=MESH)
        signals += 1

    for copy in loads:
        copy.wait()
    lane8 = lax.broadcasted_iota(jnp.int32, (8, HALF), 1)
    lane1 = lax.broadcasted_iota(jnp.int32, (1, HALF), 1)
    for t in range(STEPS):
        bcf[t] = bcin[t].astype(jnp.float32)
    extra[...] = jnp.zeros((8, HALF), jnp.float32)
    for t in range(STEPS):
        extra[0:2, 64 + 8 * t : 72 + 8 * t] = dtin[t].astype(jnp.float32)
    for j in range(2):
        for t in range(STEPS):
            extra[j : j + 1, :] = jnp.where(
                lane1 == 88 + t, active[j, t].astype(jnp.float32), extra[j : j + 1, :]
            )
    model[...] = jnp.zeros((2, 4, 8, HALF), jnp.float32)
    for cc in range(2):
        for h in range(2):
            base = pl.multiple_of(h * 1024 + g * 2 * HALF + cc * HALF, HALF)
            for j in range(2):
                for e in range(6):
                    table = cbc if e < 3 else bcf
                    model[cc, 2 * j + h, e : e + 1, :] = table[
                        e % 3, j : j + 1, pl.ds(base, HALF)
                    ]

    def fill(p, _):
        pk[p] = model[p % 2]
        return 0

    lax.fori_loop(0, PLANE, fill, 0)
    stacks = [stack4(cx[e]) for e in range(3)]
    stacks += [stack4(xin[e].astype(jnp.float32)) for e in range(3)]
    extra_rows = jnp.concatenate([extra[0:2, :]] * 4, axis=0)
    quarter = pl.ds(pl.multiple_of(m * 512, 512), 512)
    stacks_bc = [stack4((cbc if e < 3 else bcf)[e % 3, :, quarter]) for e in range(6)]
    for r in range(8):
        row = jnp.zeros((8, HALF), jnp.float32)
        for e in range(6):
            moved = pltpu.roll(stacks_bc[e], (FEW * (e - r)) % HALF, 1)
            row = jnp.where(lane8 // FEW == e, moved, row)
        for a in range(4):
            for j in range(2):
                pk[8 * a + r, 2 * j, 7:8, :] = row[2 * a + j : 2 * a + j + 1]
    for b in range(4):
        for h in range(2):
            row = jnp.zeros((8, HALF), jnp.float32)
            for e in range(4 * h, min(6, 4 * h + 4)):
                moved = pltpu.roll(stacks[e], (CHUNK * (e % 4 - b)) % HALF, 1)
                row = jnp.where(lane8 // CHUNK == e % 4, moved, row)
            if h:
                row = row + extra_rows
            for a in range(4):
                for j in range(2):
                    for cc in range(2):
                        p = 2 * (4 * a + b) + cc
                        pk[p, 2 * j + h, 6:7, :] = row[2 * a + j : 2 * a + j + 1]

    pl.semaphore_wait(barrier, signals)

    def lines(device):
        return pl.ds(pl.multiple_of(device * 8, 8), 8)

    def small_copy(p, source):
        return pltpu.make_async_remote_copy(
            src_ref=pk.at[p], dst_ref=buf.at[:, lines(source)],
            send_sem=pk_ss.at[p], recv_sem=pk_rs.at[source],
            device_id=(p, z), device_id_type=MESH,
        )

    def slab(qq, cc, part):
        return (
            slice(None),
            pl.ds(pl.multiple_of(qq * CHUNK + part * PART, PART), PART),
            pl.ds(pl.multiple_of(cc * HALF, HALF), HALF),
        )

    def state_copy(p, qq, cc, part, source):
        return pltpu.make_async_remote_copy(
            src_ref=ssm.at[slab(qq, cc, part)],
            dst_ref=sbufs[part].at[:, source],
            send_sem=s_ss.at[part, p], recv_sem=s_rs.at[part, source],
            device_id=(p, z), device_id_type=MESH,
        )

    own_small = pltpu.make_async_copy(pk.at[d], buf.at[:, lines(d)], local_sem.at[0])
    own_states = [
        pltpu.make_async_copy(
            ssm.at[slab(q, c, part)], sbufs[part].at[:, d], local_sem.at[1 + part]
        )
        for part in range(PARTS)
    ]
    for offset in OFFSETS:
        small_copy(at(offset)[0], d).start()
    own_small.start()
    for part in range(PARTS):
        for offset in OFFSETS:
            p, qq, cc = at(offset)
            state_copy(p, qq, cc, part, d).start()
        own_states[part].start()

    down = lax.broadcasted_iota(jnp.int32, (ROWS, ROWS), 0)
    across = lax.broadcasted_iota(jnp.int32, (ROWS, ROWS), 1)
    same = down == across
    eye = same.astype(jnp.float32)
    moves = []
    picks = []
    for t in range(STEPS):
        dest_row = jnp.concatenate([dest[t : t + 1, :]] * 2, axis=1)
        send_row = jnp.concatenate([send[t : t + 1, :]] * 2, axis=1)
        send_col = jnp.sum(jnp.where(same, send_row, 0), axis=1, keepdims=True)
        arrives = (dest_row == down % PLANE) & (send_row == across // PLANE)
        moved = send_col == down // PLANE
        picks.append((moved & arrives) | (jnp.logical_not(moved) & same))
        moves.append(picks[t].astype(jnp.float32).astype(jnp.bfloat16))
    place2 = moves[2].astype(jnp.float32)
    place1 = dot_nn(moves[2], moves[1], None)
    place0 = dot_nn(place1.astype(jnp.bfloat16), moves[0], None)
    source = jnp.sum(jnp.where(picks[2], across, 0), axis=1, keepdims=True)
    for t in (1, 0):
        before = jnp.sum(jnp.where(picks[t], across, 0), axis=1, keepdims=True)
        before = jnp.sum(jnp.where(same, before, 0), axis=0, keepdims=True)
        source = jnp.sum(jnp.where(across == source, before, 0), axis=1, keepdims=True)
    source = jnp.sum(jnp.where(same, source, 0), axis=0, keepdims=True)
    source = jnp.minimum(jnp.maximum(source, 0), ROWS - 1)
    upper = (source >= PLANE).astype(jnp.int32)
    sidx_v[...] = jnp.zeros((8, HALF), jnp.int32)
    sidx_v[0:1, 0:ROWS] = upper
    sidx_v[1:2, 0:ROWS] = source - upper * PLANE
    to_scalar = pltpu.make_async_copy(sidx_v, sidx_s, local_sem.at[3])
    to_scalar.start()
    places = (place1, place2, eye)

    own_small.wait()
    for offset in OFFSETS:
        p = at(offset)[0]
        small_copy(p, p).wait_recv()

    def entry(e):
        return jnp.concatenate(
            [
                jnp.concatenate(
                    [buf[j * 2 + h, pl.ds(e, PLANE, stride=8), :] for j in range(2)], axis=0
                )
                for h in range(2)
            ],
            axis=1,
        )

    packed = entry(6)
    turned = jnp.transpose(packed)
    marks = turned[192:224]
    first = dot_nt(turned[0:96], place0)
    fresh_x = []
    fresh_marks = []
    for t in range(STEPS):
        new = turned[96 + CHUNK * t : 96 + CHUNK * (t + 1)]
        fresh_x.append(new if t == 2 else dot_nt(new, places[t]))
        fresh_marks.append(marks if t == 2 else dot_nt(marks, places[t]))
    window = [first[CHUNK * k : CHUNK * (k + 1)] for k in range(3)]
    pick = (
        lax.broadcasted_iota(jnp.int32, (CHUNK, HALF), 0) + CHUNK * (q % 4)
        == lax.broadcasted_iota(jnp.int32, (CHUNK, HALF), 1)
    ).astype(jnp.float32)
    quarter = wx[:, pl.ds(pl.multiple_of(q // 4 * HALF, HALF), HALF)]
    weights = dot_nt(
        pick, jnp.concatenate([quarter, jnp.zeros((4, HALF), jnp.float32)], axis=0)
    )
    of_head = lax.broadcasted_iota(jnp.int32, (8, ROWS), 0) == q // 2
    head = q // 2
    bias = dt_bias[head]
    rate = a_rate[head]
    skip = jnp.where(c == 0, d_skip[head], 0.0)
    live_cols = []
    skipped = []
    for t in range(STEPS):
        new = fresh_x[t]
        raw = jnp.where(of_head, fresh_marks[t][8 * t : 8 * t + 8], 0.0)
        raw = jnp.sum(raw, axis=0, keepdims=True) + bias
        live = fresh_marks[t][24 + t : 25 + t]
        delta = jnp.maximum(raw, 0.0) + jnp.log1p(jnp.exp(-jnp.abs(raw)))
        decay = jnp.exp(-delta * rate)
        mixed_x = silu(
            window[0] * weights[:, 0:1]
            + window[1] * weights[:, 1:2]
            + window[2] * weights[:, 2:3]
            + new * weights[:, 3:4]
        )
        on = jnp.broadcast_to(live, (CHUNK, ROWS)) > 0.5
        dxs[t, :, 0:ROWS] = jnp.where(on, delta * mixed_x, 0.0)
        decs[t, :, 0:ROWS] = jnp.broadcast_to(
            jnp.where(live > 0.5, decay, 1.0), (8, ROWS)
        )
        skipped.append(skip * mixed_x)
        window = [
            jnp.where(on, window[1], window[0]),
            jnp.where(on, window[2], window[1]),
            jnp.where(on, new, window[2]),
        ]
        live_cols.append(column(live, same))

    window_bc = [dot_nn(place0, entry(e)) for e in range(3)]
    w_bc = jnp.concatenate(
        [
            wbc[:, pl.ds(pl.multiple_of(h * 1024 + g * 2 * HALF + c * HALF, HALF), HALF)]
            for h in range(2)
        ],
        axis=1,
    )
    few = jnp.concatenate(
        [buf[2 * j, pl.ds(7, PLANE, stride=8), :] for j in range(2)], axis=0
    )
    window_all = dot_nn(place0, few)[:, 0 : 3 * FEW]
    for t in range(STEPS):
        new = entry(3 + t)
        if t < 2:
            new = dot_nn(places[t], new)
        both = silu(
            window_bc[0] * w_bc[0:1]
            + window_bc[1] * w_bc[1:2]
            + window_bc[2] * w_bc[2:3]
            + new * w_bc[3:4]
        )
        mixed[t, 0] = both[:, :HALF]
        mixed[t, 1] = both[:, HALF:]
        if t < 2:
            on = jnp.broadcast_to(live_cols[t], (ROWS, 2 * HALF)) > 0.5
            window_bc = [
                jnp.where(on, window_bc[1], window_bc[0]),
                jnp.where(on, window_bc[2], window_bc[1]),
                jnp.where(on, new, window_bc[2]),
            ]
        new = few if t == 2 else dot_nn(places[t], few)
        new = new[:, FEW * (3 + t) : FEW * (4 + t)]
        on = jnp.broadcast_to(live_cols[t], (ROWS, 3 * FEW)) > 0.5
        window_all = jnp.where(
            on, jnp.concatenate([window_all[:, FEW:], new], axis=1), window_all
        )

    def final_copy(p, part, source):
        return pltpu.make_async_remote_copy(
            src_ref=obuf.at[part, :, p], dst_ref=out_s.at[slab(source // 2, source % 2, part)],
            send_sem=o_ss.at[part, p], recv_sem=o_rs.at[part, source],
            device_id=(p, z), device_id_type=MESH,
        )

    own_finals = [
        pltpu.make_async_copy(
            obuf.at[part, :, d], out_s.at[slab(q, c, part)], local_sem.at[4 + part]
        )
        for part in range(PARTS)
    ]
    lane = lax.broadcasted_iota(jnp.int32, (PART, HALF), 1)
    zero = jnp.zeros((PART, HALF), jnp.float32)
    to_scalar.wait()
    reads = []

    wide_lane = lax.broadcasted_iota(jnp.int32, (CHUNK, HALF), 1)

    def push(i, _):
        for k in range(4):
            f = i * 4 + k
            for t in range(STEPS):
                dx = jnp.where(wide_lane == f, dxs[t], 0.0)
                dx = jnp.sum(dx, axis=1, keepdims=True)
                dec = jnp.where(lane8 == f, decs[t], 0.0)
                dec = jnp.sum(dec, axis=1, keepdims=True)
                pushes[f, t] = dx * mixed[t, 0, pl.ds(f, 1), :]
                fades[f, t] = jnp.broadcast_to(dec, (8, HALF))
        return 0

    lax.fori_loop(0, ROWS // 4, push, 0)

    def advance_part(part):
        def advance(j, dd, ys):
            f = j * PLANE + dd
            state = sbufs[part][sidx_s[0, f], sidx_s[1, f]].reshape(PART // 8, 8, HALF)
            here = lane == f
            out = []
            for t in range(STEPS):
                c_row = mixed[t, 1, pl.ds(f, 1), :]
                added = pushes[f, t, part * PART : (part + 1) * PART, :]
                state = state * fades[f, t][None] + added.reshape(PART // 8, 8, HALF)
                read = jnp.sum(state.reshape(PART, HALF) * c_row, axis=1, keepdims=True)
                out.append(jnp.where(here, read, ys[t]))
            obuf[part, j, dd] = state.reshape(PART, HALF)
            return tuple(out)

        def advance_some(i, ys):
            for k in range(2):
                for j in range(2):
                    ys = advance(j, i * 2 + k, ys)
            return ys

        return lax.fori_loop(0, PLANE // 2, advance_some, (zero,) * STEPS)

    for part in range(PARTS):
        own_states[part].wait()
        for offset in OFFSETS:
            p, qq, cc = at(offset)
            state_copy(p, qq, cc, part, p).wait_recv()
        reads.append(advance_part(part))
        if part < PARTS - 1:
            for offset in OFFSETS:
                final_copy(at(offset)[0], part, d).start()
            own_finals[part].start()

    pieces = [None] * 6
    for t in range(STEPS):
        read = jnp.concatenate([part[t][:, 0:ROWS] for part in reads], axis=0)
        read = read + skipped[t]
        back = eye if t == 2 else dot_nt(eye, places[t])
        pieces[t] = dot_nt(back, read)
        pieces[3 + t] = dot_nt(eye, window[t])
    for n in range(6):
        lo = CHUNK * (n % 4)
        flat[n // 4, :, lo : lo + CHUNK] = pieces[n]
    flat[1, :, 64 : 64 + 3 * FEW] = window_all
    flat[1, :, 64 + 3 * FEW :] = jnp.zeros((ROWS, 64 - 3 * FEW), jnp.float32)

    def spread_rows(dd, _):
        for j in range(2):
            for n in range(2):
                ysend[dd, j : j + 1, HALF * n : HALF * (n + 1)] = flat[
                    n, pl.ds(j * PLANE + dd, 1), :
                ]
        return 0

    lax.fori_loop(0, PLANE, spread_rows, 0)

    def read_copy(p, source):
        return pltpu.make_async_remote_copy(
            src_ref=ysend.at[p], dst_ref=yrecv.at[source],
            send_sem=y_ss.at[p], recv_sem=y_rs.at[source],
            device_id=(p, z), device_id_type=MESH,
        )

    own_read = pltpu.make_async_copy(ysend.at[d], yrecv.at[d], local_sem.at[6])
    for offset in OFFSETS:
        read_copy(at(offset)[0], d).start()
    own_read.start()
    for offset in OFFSETS:
        final_copy(at(offset)[0], PARTS - 1, d).start()
    own_finals[PARTS - 1].start()

    own_read.wait()
    for offset in OFFSETS:
        p = at(offset)[0]
        read_copy(p, p).wait_recv()

    def gather4(h, b, cc):
        return jnp.concatenate(
            [
                yrecv[2 * (4 * a + b) + cc, :, HALF * h : HALF * (h + 1)]
                for a in range(4)
            ],
            axis=0,
        )

    wide = [jnp.zeros((8, HALF), jnp.float32)] * 6
    for b in range(4):
        tiles = [gather4(0, b, 0), gather4(1, b, 0)]
        summed = tiles[0] + gather4(0, b, 1)
        for e in range(6):
            tile = summed if e < 3 else tiles[e // 4]
            moved = pltpu.roll(tile, (CHUNK * (b - e % 4)) % HALF, 1)
            wide[e] = jnp.where(lane8 // CHUNK == b, moved, wide[e])
    closing = [jnp.zeros((8, HALF), jnp.float32)] * 3
    for r in range(8):
        tile = jnp.concatenate(
            [yrecv[8 * a + r, :, HALF : 2 * HALF] for a in range(4)], axis=0
        )
        for e in range(3):
            moved = pltpu.roll(tile, (FEW * (r - e) - 64) % HALF, 1)
            closing[e] = jnp.where(lane8 // FEW == r, moved, closing[e])
    for e in range(3):
        ends[m, e] = closing[e]
    gated = []
    squares = jnp.zeros((8, HALF), jnp.float32)
    for t in range(STEPS):
        gated.append(wide[t] * silu(stack4(zin[t].astype(jnp.float32))))
        part = jnp.sum(gated[t] * gated[t], axis=1, keepdims=True)
        squares = jnp.where(lane8 == t, part, squares)
    sqsend[...] = squares
    sq_copies = []
    for n, peer in enumerate(norm_peers):
        copy = pltpu.make_async_remote_copy(
            src_ref=sqsend, dst_ref=sqrecv.at[n],
            send_sem=q_ss.at[n], recv_sem=q_rs.at[n],
            device_id=peer, device_id_type=MESH,
        )
        copy.start()
        sq_copies.append(copy)
        copy = pltpu.make_async_remote_copy(
            src_ref=ends.at[m], dst_ref=ends.at[m],
            send_sem=q_ss.at[3 + n], recv_sem=q_rs.at[3 + n],
            device_id=peer, device_id_type=MESH,
        )
        copy.start()
        sq_copies.append(copy)
    for a in range(4):
        for e in range(3):
            out_x[e, :, HALF * a : HALF * (a + 1)] = wide[3 + e][2 * a : 2 * a + 2]
    for copy in sq_copies:
        copy.wait()
    for n in range(SIDE):
        for e in range(3):
            for a in range(4):
                lo = 512 * n + HALF * a
                out_bc[e, :, lo : lo + HALF] = ends[n, e, 2 * a : 2 * a + 2, :]
    total = sqsend[...] + sqrecv[0] + sqrecv[1] + sqrecv[2]
    even = lax.broadcasted_iota(jnp.int32, (8, HALF), 0) % 2 == 0
    gains = jnp.concatenate([gain[n // 2 : n // 2 + 1, :] for n in range(8)], axis=0)
    for t in range(STEPS):
        col = jnp.sum(jnp.where(lane8 == t, total, 0.0), axis=1, keepdims=True)
        col = jnp.broadcast_to(col, (8, HALF))
        of_even = jnp.sum(jnp.where(even, col, 0.0), axis=0, keepdims=True)
        of_odd = jnp.sum(jnp.where(even, 0.0, col), axis=0, keepdims=True)
        factor = lax.rsqrt(jnp.where(even, of_even, of_odd) / NORM_WIDTH + 1e-05)
        on = jnp.where(even, active[0, t], active[1, t]) > 0
        normed = jnp.where(on, gated[t] * factor * gains, 0.0)
        for a in range(4):
            out_m[t, :, HALF * a : HALF * (a + 1)] = normed[2 * a : 2 * a + 2]

    for part in range(PARTS):
        own_finals[part].wait()
        for offset in OFFSETS:
            p = at(offset)[0]
            final_copy(p, part, p).wait_recv()
    for offset in OFFSETS:
        p, qq, cc = at(offset)
        small_copy(p, d).wait_send()
        read_copy(p, d).wait_send()
        for part in range(PARTS):
            state_copy(p, qq, cc, part, d).wait_send()
            final_copy(p, part, d).wait_send()


def finish(*refs):
    given, outs, held, mixer, sems = refs[:4], refs[4:8], refs[8:12], refs[12], refs[13]
    loads = [
        pltpu.make_async_copy(source, target, sems.at[0, n])
        for n, (source, target) in enumerate(zip(given, held))
    ]
    for copy in loads:
        copy.start()
    stores = [
        pltpu.make_async_copy(source, target, sems.at[1, n])
        for n, (source, target) in enumerate(zip((*held[:3], mixer), outs))
    ]
    for n in (1, 2):
        loads[n].wait()
        stores[n].start()
    loads[3].wait()
    mixer[...] = held[3][...].astype(jnp.bfloat16)
    stores[3].start()
    loads[0].wait()
    stores[0].start()
    for copy in stores:
        copy.wait()


def local(
    ssm_state, conv_x, conv_bc, x_in, bc_in, z_in, dt_in, conv_w_x, conv_w_bc,
    dt_bias, a_rate, d_skip, norm_gain, send_slot, dest_group, active,
):
    f32 = jnp.float32
    vmem = pl.BlockSpec(memory_space=pltpu.VMEM)
    hbm = pl.BlockSpec(memory_space=pltpu.HBM)
    dma = pltpu.SemaphoreType.DMA
    shapes = [
        jax.ShapeDtypeStruct((2, 512, 256), f32),
        jax.ShapeDtypeStruct((STEPS, 2, 512), f32),
        jax.ShapeDtypeStruct((3, 2, 512), f32),
        jax.ShapeDtypeStruct((3, 2, 2048), f32),
    ]
    state, mix, final_x, final_bc = pl.pallas_call(
        kernel,
        out_shape=tuple(shapes),
        in_specs=[hbm] * (1 + FIXED),
        out_specs=(hbm, vmem, vmem, vmem),
        scratch_shapes=[
            pltpu.VMEM((3, 2, 512), f32),
            pltpu.VMEM((STEPS, 2, 512), jnp.bfloat16),
            pltpu.VMEM((3, 2, 2048), f32),
            pltpu.VMEM((STEPS, 2, 2048), jnp.bfloat16),
            pltpu.VMEM((STEPS, 2, 512), jnp.bfloat16),
            pltpu.VMEM((STEPS, 2, 8), jnp.bfloat16),
            pltpu.VMEM((4, 512), f32),
            pltpu.VMEM((4, 2048), f32),
            pltpu.VMEM((4, HALF), f32),
            pltpu.VMEM((STEPS, PLANE), jnp.int32),
            pltpu.VMEM((STEPS, PLANE), jnp.int32),
            pltpu.SMEM((2, STEPS), jnp.int32),
            pltpu.SMEM((8,), f32),
            pltpu.SMEM((8,), f32),
            pltpu.SMEM((8,), f32),
            dma((16,)),
            pltpu.VMEM((PLANE, 4, 8, HALF), f32),
            pltpu.VMEM((4, PLANE * 8, HALF), f32),
            pltpu.VMEM((2, PLANE, PART, HALF), f32),
            pltpu.VMEM((2, PLANE, PART, HALF), f32),
            pltpu.VMEM((PARTS, 2, PLANE, PART, HALF), f32),
            pltpu.VMEM((STEPS, CHUNK, HALF), f32),
            pltpu.VMEM((STEPS, 8, HALF), f32),
            pltpu.VMEM((STEPS, 2, ROWS, HALF), f32),
            pltpu.VMEM((2, ROWS, HALF), f32),
            pltpu.VMEM((PLANE, 2, 256), f32),
            pltpu.VMEM((PLANE, 2, 256), f32),
            pltpu.VMEM((SIDE, 3, 8, HALF), f32),
            pltpu.VMEM((ROWS, STEPS, CHUNK, HALF), f32),
            pltpu.VMEM((ROWS, STEPS, 8, HALF), f32),
            pltpu.VMEM((8, HALF), f32),
            pltpu.VMEM((3, 8, HALF), f32),
            pltpu.VMEM((8, HALF), jnp.int32),
            pltpu.VMEM((STEPS, 2, 2048), f32),
            pltpu.VMEM((2, 4, 8, HALF), f32),
            pltpu.VMEM((8, HALF), f32),
            pltpu.SMEM((8, HALF), jnp.int32),
            dma((PLANE,)), dma((PLANE,)),
            dma((PARTS, PLANE)), dma((PARTS, PLANE)),
            dma((PARTS, PLANE)), dma((PARTS, PLANE)),
            dma((PLANE,)), dma((PLANE,)),
            dma((8,)), dma((8,)),
            dma((8,)),
        ],
        compiler_params=pltpu.CompilerParams(
            collective_id=0, has_side_effects=True, vmem_limit_bytes=VMEM_BYTES
        ),
    )(
        ssm_state.reshape(2, 512, 256), jnp.swapaxes(conv_x, 0, 1), x_in,
        jnp.swapaxes(conv_bc, 0, 1), bc_in, z_in, dt_in, conv_w_x, conv_w_bc,
        norm_gain.reshape(4, HALF), dest_group, send_slot, jnp.transpose(active),
        dt_bias, a_rate, d_skip,
    )
    bits = jax.ShapeDtypeStruct((STEPS, 2, 512), jnp.bfloat16)
    state, final_x, final_bc, mixer = pl.pallas_call(
        finish,
        out_shape=(shapes[0], shapes[2], shapes[3], bits),
        in_specs=[hbm] * 4,
        out_specs=(hbm,) * 4,
        scratch_shapes=[
            pltpu.VMEM(shapes[n].shape, f32) for n in (0, 2, 3, 1)
        ] + [pltpu.VMEM(bits.shape, jnp.bfloat16), dma((2, 4))],
        compiler_params=pltpu.CompilerParams(vmem_limit_bytes=VMEM_BYTES),
    )(state, final_x, final_bc, mix)
    return (
        mixer,
        state.reshape(ssm_state.shape),
        jnp.swapaxes(final_x, 0, 1),
        jnp.swapaxes(final_bc, 0, 1),
    )


def solution(mesh):
    return jax.shard_map(
        local,
        mesh=mesh,
        in_specs=(
            P("dp", "tensor", None, None),
            P("dp", None, "tensor"),
            P("dp", None, None),
            P(None, "dp", "tensor"),
            P(None, "dp", None),
            P(None, "dp", "tensor"),
            P(None, "dp", "tensor"),
            P(None, "tensor"),
            P(),
            P("tensor"),
            P("tensor"),
            P("tensor"),
            P("tensor"),
            P(),
            P(),
            P(None, "dp"),
        ),
        out_specs=(
            P(None, "dp", "tensor"),
            P("dp", "tensor", None, None),
            P("dp", None, "tensor"),
            P("dp", None, None),
        ),
        check_vma=False,
    )
```

```python
import jax
import jax.numpy as jnp
from jax import lax
from jax.experimental import pallas as pl
from jax.experimental.pallas import tpu as pltpu
from jax.sharding import PartitionSpec as P

MESH = pl.DeviceIdType.MESH
HIGH = lax.Precision.HIGHEST
STEPS = 3
SIDE = 4
CHIPS = 16
PLANE = 32
ROWS = 64
CHUNK = 32
FIXED = 15
FEW = 16
VMEM_BYTES = 63 * 2**20
PARTS = 2
PART = CHUNK // PARTS
HALF = 128
TENSOR = 16
GROUPS = 4
NORM_WIDTH = 2048

HOPS = (
    (2, 2), (2, 1), (1, 2), (2, 3), (3, 2), (2, 0), (0, 2), (1, 1),
    (3, 3), (1, 3), (3, 1), (1, 0), (0, 1), (3, 0), (0, 3), (0, 0),
)
OFFSETS = tuple(
    (kc, kx, ky) for kx, ky in HOPS for kc in (0, 1) if (kc, kx, ky) != (0, 0, 0)
)


def dot_nt(a, b, precision=HIGH):
    return lax.dot_general(
        a, b, (((1,), (1,)), ((), ())), precision=precision,
        preferred_element_type=jnp.float32,
    )


def dot_nn(a, b, precision=HIGH):
    return lax.dot_general(
        a, b, (((1,), (0,)), ((), ())), precision=precision,
        preferred_element_type=jnp.float32,
    )


def stack4(v):
    return jnp.concatenate([v[:, HALF * a : HALF * (a + 1)] for a in range(4)], axis=0)


def silu(v):
    return v / (1.0 + jnp.exp(-v))


def column(row_values, same):
    return jnp.sum(jnp.where(same, row_values, 0.0), axis=1, keepdims=True)


def kernel(
    ssm, *refs,
):
    given, refs = refs[:FIXED], refs[FIXED:]
    outs, held, refs = refs[:4], refs[4 : 4 + FIXED], refs[4 + FIXED :]
    run(ssm, *held, *outs, given, held, *refs)


def run(
    ssm, cx, xin, cbc, bcin, zin, dtin, wx, wbc, gain, dest, send,
    active, dt_bias, a_rate, d_skip,
    out_s, out_m, out_x, out_bc, given, held, in_sem,
    pk, buf, sbuf0, sbuf1, obuf, dxs, decs, mixed, flat, ysend, yrecv, ends, pushes, fades,
    sqsend, sqrecv, sidx_v, bcf, model, extra, sidx_s,
    pk_ss, pk_rs, s_ss, s_rs, o_ss, o_rs, y_ss, y_rs, q_ss, q_rs, local_sem,
):
    sbufs = (sbuf0, sbuf1)
    d = lax.axis_index("dp")
    z = lax.axis_index("tensor")
    c = d % 2
    q = d // 2
    x = q % SIDE
    y = q // SIDE
    g = z // SIDE
    m = z % SIDE

    def at(offset):
        kc, kx, ky = offset
        cc = (c + kc) % 2
        qq = ((y + ky) % SIDE) * SIDE + (x + kx) % SIDE
        return qq * 2 + cc, qq, cc

    norm_peers = [(d, g * SIDE + (m + i) % SIDE) for i in range(1, SIDE)]

    loads = [
        pltpu.make_async_copy(source, target, in_sem.at[n])
        for n, (source, target) in enumerate(zip(given, held))
    ]
    barrier = pltpu.get_barrier_semaphore()
    signals = 0
    for offset in OFFSETS:
        pl.semaphore_signal(barrier, inc=1, device_id=(at(offset)[0], z), device_id_type=MESH)
        signals += 1
    for peer in norm_peers:
        pl.semaphore_signal(barrier, inc=1, device_id=peer, device_id_type=MESH)
        signals += 1

    for copy in loads:
        copy.start()

    for copy in loads:
        copy.wait()
    lane8 = lax.broadcasted_iota(jnp.int32, (8, HALF), 1)
    lane1 = lax.broadcasted_iota(jnp.int32, (1, HALF), 1)
    for t in range(STEPS):
        bcf[t] = bcin[t].astype(jnp.float32)
    extra[...] = jnp.zeros((8, HALF), jnp.float32)
    for t in range(STEPS):
        extra[0:2, 64 + 8 * t : 72 + 8 * t] = dtin[t].astype(jnp.float32)
    for j in range(2):
        for t in range(STEPS):
            extra[j : j + 1, :] = jnp.where(
                lane1 == 88 + t, active[j, t].astype(jnp.float32), extra[j : j + 1, :]
            )
    model[...] = jnp.zeros((2, 4, 8, HALF), jnp.float32)
    for cc in range(2):
        for h in range(2):
            base = pl.multiple_of(h * 1024 + g * 2 * HALF + cc * HALF, HALF)
            for j in range(2):
                for e in range(6):
                    table = cbc if e < 3 else bcf
                    model[cc, 2 * j + h, e : e + 1, :] = table[
                        e % 3, j : j + 1, pl.ds(base, HALF)
                    ]

    def fill(p, _):
        pk[p] = model[p % 2]
        return 0

    lax.fori_loop(0, PLANE, fill, 0)
    stacks = [stack4(cx[e]) for e in range(3)]
    stacks += [stack4(xin[e].astype(jnp.float32)) for e in range(3)]
    extra_rows = jnp.concatenate([extra[0:2, :]] * 4, axis=0)
    quarter = pl.ds(pl.multiple_of(m * 512, 512), 512)
    stacks_bc = [stack4((cbc if e < 3 else bcf)[e % 3, :, quarter]) for e in range(6)]
    for r in range(8):
        row = jnp.zeros((8, HALF), jnp.float32)
        for e in range(6):
            moved = pltpu.roll(stacks_bc[e], (FEW * (e - r)) % HALF, 1)
            row = jnp.where(lane8 // FEW == e, moved, row)
        for a in range(4):
            for j in range(2):
                pk[8 * a + r, 2 * j, 7:8, :] = row[2 * a + j : 2 * a + j + 1]
    for b in range(4):
        for h in range(2):
            row = jnp.zeros((8, HALF), jnp.float32)
            for e in range(4 * h, min(6, 4 * h + 4)):
                moved = pltpu.roll(stacks[e], (CHUNK * (e % 4 - b)) % HALF, 1)
                row = jnp.where(lane8 // CHUNK == e % 4, moved, row)
            if h:
                row = row + extra_rows
            for a in range(4):
                for j in range(2):
                    for cc in range(2):
                        p = 2 * (4 * a + b) + cc
                        pk[p, 2 * j + h, 6:7, :] = row[2 * a + j : 2 * a + j + 1]

    pl.semaphore_wait(barrier, signals)

    def lines(device):
        return pl.ds(pl.multiple_of(device * 8, 8), 8)

    def small_copy(p, source):
        return pltpu.make_async_remote_copy(
            src_ref=pk.at[p], dst_ref=buf.at[:, lines(source)],
            send_sem=pk_ss.at[p], recv_sem=pk_rs.at[source],
            device_id=(p, z), device_id_type=MESH,
        )

    def slab(qq, cc, part):
        return (
            slice(None),
            pl.ds(pl.multiple_of(qq * CHUNK + part * PART, PART), PART),
            pl.ds(pl.multiple_of(cc * HALF, HALF), HALF),
        )

    def state_copy(p, qq, cc, part, source):
        return pltpu.make_async_remote_copy(
            src_ref=ssm.at[slab(qq, cc, part)],
            dst_ref=sbufs[part].at[:, source],
            send_sem=s_ss.at[part, p], recv_sem=s_rs.at[part, source],
            device_id=(p, z), device_id_type=MESH,
        )

    own_small = pltpu.make_async_copy(pk.at[d], buf.at[:, lines(d)], local_sem.at[0])
    own_states = [
        pltpu.make_async_copy(
            ssm.at[slab(q, c, part)], sbufs[part].at[:, d], local_sem.at[1 + part]
        )
        for part in range(PARTS)
    ]
    for offset in OFFSETS:
        small_copy(at(offset)[0], d).start()
    own_small.start()
    for part in range(PARTS):
        for offset in OFFSETS:
            p, qq, cc = at(offset)
            state_copy(p, qq, cc, part, d).start()
        own_states[part].start()

    down = lax.broadcasted_iota(jnp.int32, (ROWS, ROWS), 0)
    across = lax.broadcasted_iota(jnp.int32, (ROWS, ROWS), 1)
    same = down == across
    eye = same.astype(jnp.float32)
    moves = []
    picks = []
    for t in range(STEPS):
        dest_row = jnp.concatenate([dest[t : t + 1, :]] * 2, axis=1)
        send_row = jnp.concatenate([send[t : t + 1, :]] * 2, axis=1)
        send_col = jnp.sum(jnp.where(same, send_row, 0), axis=1, keepdims=True)
        arrives = (dest_row == down % PLANE) & (send_row == across // PLANE)
        moved = send_col == down // PLANE
        picks.append((moved & arrives) | (jnp.logical_not(moved) & same))
        moves.append(picks[t].astype(jnp.float32).astype(jnp.bfloat16))
    place2 = moves[2].astype(jnp.float32)
    place1 = dot_nn(moves[2], moves[1], None)
    place0 = dot_nn(place1.astype(jnp.bfloat16), moves[0], None)
    source = jnp.sum(jnp.where(picks[2], across, 0), axis=1, keepdims=True)
    for t in (1, 0):
        before = jnp.sum(jnp.where(picks[t], across, 0), axis=1, keepdims=True)
        before = jnp.sum(jnp.where(same, before, 0), axis=0, keepdims=True)
        source = jnp.sum(jnp.where(across == source, before, 0), axis=1, keepdims=True)
    source = jnp.sum(jnp.where(same, source, 0), axis=0, keepdims=True)
    source = jnp.minimum(jnp.maximum(source, 0), ROWS - 1)
    upper = (source >= PLANE).astype(jnp.int32)
    sidx_v[...] = jnp.zeros((8, HALF), jnp.int32)
    sidx_v[0:1, 0:ROWS] = upper
    sidx_v[1:2, 0:ROWS] = source - upper * PLANE
    to_scalar = pltpu.make_async_copy(sidx_v, sidx_s, local_sem.at[3])
    to_scalar.start()
    places = (place1, place2, eye)

    own_small.wait()
    for offset in OFFSETS:
        p = at(offset)[0]
        small_copy(p, p).wait_recv()

    def entry(e):
        return jnp.concatenate(
            [
                jnp.concatenate(
                    [buf[j * 2 + h, pl.ds(e, PLANE, stride=8), :] for j in range(2)], axis=0
                )
                for h in range(2)
            ],
            axis=1,
        )

    packed = entry(6)
    turned = jnp.transpose(packed)
    marks = turned[192:224]
    first = dot_nt(turned[0:96], place0)
    fresh_x = []
    fresh_marks = []
    for t in range(STEPS):
        new = turned[96 + CHUNK * t : 96 + CHUNK * (t + 1)]
        fresh_x.append(new if t == 2 else dot_nt(new, places[t]))
        fresh_marks.append(marks if t == 2 else dot_nt(marks, places[t]))
    window = [first[CHUNK * k : CHUNK * (k + 1)] for k in range(3)]
    pick = (
        lax.broadcasted_iota(jnp.int32, (CHUNK, HALF), 0) + CHUNK * (q % 4)
        == lax.broadcasted_iota(jnp.int32, (CHUNK, HALF), 1)
    ).astype(jnp.float32)
    quarter = wx[:, pl.ds(pl.multiple_of(q // 4 * HALF, HALF), HALF)]
    weights = dot_nt(
        pick, jnp.concatenate([quarter, jnp.zeros((4, HALF), jnp.float32)], axis=0)
    )
    of_head = lax.broadcasted_iota(jnp.int32, (8, ROWS), 0) == q // 2
    head = q // 2
    bias = dt_bias[head]
    rate = a_rate[head]
    skip = jnp.where(c == 0, d_skip[head], 0.0)
    live_cols = []
    skipped = []
    for t in range(STEPS):
        new = fresh_x[t]
        raw = jnp.where(of_head, fresh_marks[t][8 * t : 8 * t + 8], 0.0)
        raw = jnp.sum(raw, axis=0, keepdims=True) + bias
        live = fresh_marks[t][24 + t : 25 + t]
        delta = jnp.maximum(raw, 0.0) + jnp.log1p(jnp.exp(-jnp.abs(raw)))
        decay = jnp.exp(-delta * rate)
        mixed_x = silu(
            window[0] * weights[:, 0:1]
            + window[1] * weights[:, 1:2]
            + window[2] * weights[:, 2:3]
            + new * weights[:, 3:4]
        )
        on = jnp.broadcast_to(live, (CHUNK, ROWS)) > 0.5
        dxs[t, :, 0:ROWS] = jnp.where(on, delta * mixed_x, 0.0)
        decs[t, :, 0:ROWS] = jnp.broadcast_to(
            jnp.where(live > 0.5, decay, 1.0), (8, ROWS)
        )
        skipped.append(skip * mixed_x)
        window = [
            jnp.where(on, window[1], window[0]),
            jnp.where(on, window[2], window[1]),
            jnp.where(on, new, window[2]),
        ]
        live_cols.append(column(live, same))

    window_bc = [dot_nn(place0, entry(e)) for e in range(3)]
    w_bc = jnp.concatenate(
        [
            wbc[:, pl.ds(pl.multiple_of(h * 1024 + g * 2 * HALF + c * HALF, HALF), HALF)]
            for h in range(2)
        ],
        axis=1,
    )
    few = jnp.concatenate(
        [buf[2 * j, pl.ds(7, PLANE, stride=8), :] for j in range(2)], axis=0
    )
    window_all = dot_nn(place0, few)[:, 0 : 3 * FEW]
    for t in range(STEPS):
        new = entry(3 + t)
        if t < 2:
            new = dot_nn(places[t], new)
        both = silu(
            window_bc[0] * w_bc[0:1]
            + window_bc[1] * w_bc[1:2]
            + window_bc[2] * w_bc[2:3]
            + new * w_bc[3:4]
        )
        mixed[t, 0] = both[:, :HALF]
        mixed[t, 1] = both[:, HALF:]
        if t < 2:
            on = jnp.broadcast_to(live_cols[t], (ROWS, 2 * HALF)) > 0.5
            window_bc = [
                jnp.where(on, window_bc[1], window_bc[0]),
                jnp.where(on, window_bc[2], window_bc[1]),
                jnp.where(on, new, window_bc[2]),
            ]
        new = few if t == 2 else dot_nn(places[t], few)
        new = new[:, FEW * (3 + t) : FEW * (4 + t)]
        on = jnp.broadcast_to(live_cols[t], (ROWS, 3 * FEW)) > 0.5
        window_all = jnp.where(
            on, jnp.concatenate([window_all[:, FEW:], new], axis=1), window_all
        )

    def final_copy(p, part, source):
        return pltpu.make_async_remote_copy(
            src_ref=obuf.at[part, :, p], dst_ref=out_s.at[slab(source // 2, source % 2, part)],
            send_sem=o_ss.at[part, p], recv_sem=o_rs.at[part, source],
            device_id=(p, z), device_id_type=MESH,
        )

    own_finals = [
        pltpu.make_async_copy(
            obuf.at[part, :, d], out_s.at[slab(q, c, part)], local_sem.at[4 + part]
        )
        for part in range(PARTS)
    ]
    lane = lax.broadcasted_iota(jnp.int32, (PART, HALF), 1)
    zero = jnp.zeros((PART, HALF), jnp.float32)
    to_scalar.wait()
    reads = []

    backs = [eye if t == 2 else dot_nt(eye, places[t]) for t in range(STEPS)]
    for t in range(STEPS):
        lo = CHUNK * ((3 + t) % 4)
        flat[(3 + t) // 4, :, lo : lo + CHUNK] = dot_nt(eye, window[t])
    flat[1, :, 64 : 64 + 3 * FEW] = window_all
    flat[1, :, 64 + 3 * FEW :] = jnp.zeros((ROWS, 64 - 3 * FEW), jnp.float32)

    def spread_rows(n):
        def spread(dd, _):
            for j in range(2):
                ysend[dd, j : j + 1, HALF * n : HALF * (n + 1)] = flat[
                    n, pl.ds(j * PLANE + dd, 1), :
                ]
            return 0

        lax.fori_loop(0, PLANE, spread, 0)

    spread_rows(1)

    wide_lane = lax.broadcasted_iota(jnp.int32, (CHUNK, HALF), 1)

    def push(i, _):
        for k in range(4):
            f = i * 4 + k
            for t in range(STEPS):
                dx = jnp.where(wide_lane == f, dxs[t], 0.0)
                dx = jnp.sum(dx, axis=1, keepdims=True)
                dec = jnp.where(lane8 == f, decs[t], 0.0)
                dec = jnp.sum(dec, axis=1, keepdims=True)
                pushes[f, t] = dx * mixed[t, 0, pl.ds(f, 1), :]
                fades[f, t] = jnp.broadcast_to(dec, (8, HALF))
        return 0

    lax.fori_loop(0, ROWS // 4, push, 0)

    def advance_part(part):
        def advance(j, dd, ys):
            f = j * PLANE + dd
            state = sbufs[part][sidx_s[0, f], sidx_s[1, f]].reshape(PART // 8, 8, HALF)
            here = lane == f
            out = []
            for t in range(STEPS):
                c_row = mixed[t, 1, pl.ds(f, 1), :]
                added = pushes[f, t, part * PART : (part + 1) * PART, :]
                state = state * fades[f, t][None] + added.reshape(PART // 8, 8, HALF)
                read = jnp.sum(state.reshape(PART, HALF) * c_row, axis=1, keepdims=True)
                out.append(jnp.where(here, read, ys[t]))
            obuf[part, j, dd] = state.reshape(PART, HALF)
            return tuple(out)

        def advance_some(i, ys):
            for k in range(2):
                for j in range(2):
                    ys = advance(j, i * 2 + k, ys)
            return ys

        return lax.fori_loop(0, PLANE // 2, advance_some, (zero,) * STEPS)

    for part in range(PARTS):
        own_states[part].wait()
        for offset in OFFSETS:
            p, qq, cc = at(offset)
            state_copy(p, qq, cc, part, p).wait_recv()
        reads.append(advance_part(part))
        if part < PARTS - 1:
            for offset in OFFSETS:
                final_copy(at(offset)[0], part, d).start()
            own_finals[part].start()

    for t in range(STEPS):
        read = jnp.concatenate([part[t][:, 0:ROWS] for part in reads], axis=0)
        flat[0, :, CHUNK * t : CHUNK * (t + 1)] = dot_nt(backs[t], read + skipped[t])
    spread_rows(0)

    def read_copy(p, source):
        return pltpu.make_async_remote_copy(
            src_ref=ysend.at[p], dst_ref=yrecv.at[source],
            send_sem=y_ss.at[p], recv_sem=y_rs.at[source],
            device_id=(p, z), device_id_type=MESH,
        )

    own_read = pltpu.make_async_copy(ysend.at[d], yrecv.at[d], local_sem.at[6])
    for offset in OFFSETS:
        read_copy(at(offset)[0], d).start()
    own_read.start()
    for offset in OFFSETS:
        final_copy(at(offset)[0], PARTS - 1, d).start()
    own_finals[PARTS - 1].start()

    own_read.wait()
    for offset in OFFSETS:
        p = at(offset)[0]
        read_copy(p, p).wait_recv()

    def gather4(h, b, cc):
        return jnp.concatenate(
            [
                yrecv[2 * (4 * a + b) + cc, :, HALF * h : HALF * (h + 1)]
                for a in range(4)
            ],
            axis=0,
        )

    wide = [jnp.zeros((8, HALF), jnp.float32)] * 6
    for b in range(4):
        tiles = [gather4(0, b, 0), gather4(1, b, 0)]
        summed = tiles[0] + gather4(0, b, 1)
        for e in range(6):
            tile = summed if e < 3 else tiles[e // 4]
            moved = pltpu.roll(tile, (CHUNK * (b - e % 4)) % HALF, 1)
            wide[e] = jnp.where(lane8 // CHUNK == b, moved, wide[e])
    closing = [jnp.zeros((8, HALF), jnp.float32)] * 3
    for r in range(8):
        tile = jnp.concatenate(
            [yrecv[8 * a + r, :, HALF : 2 * HALF] for a in range(4)], axis=0
        )
        for e in range(3):
            moved = pltpu.roll(tile, (FEW * (r - e) - 64) % HALF, 1)
            closing[e] = jnp.where(lane8 // FEW == r, moved, closing[e])
    for e in range(3):
        ends[m, e] = closing[e]
    gated = []
    squares = jnp.zeros((8, HALF), jnp.float32)
    for t in range(STEPS):
        gated.append(wide[t] * silu(stack4(zin[t].astype(jnp.float32))))
        part = jnp.sum(gated[t] * gated[t], axis=1, keepdims=True)
        squares = jnp.where(lane8 == t, part, squares)
    sqsend[...] = squares
    sq_copies = []
    for n, peer in enumerate(norm_peers):
        copy = pltpu.make_async_remote_copy(
            src_ref=sqsend, dst_ref=sqrecv.at[n],
            send_sem=q_ss.at[n], recv_sem=q_rs.at[n],
            device_id=peer, device_id_type=MESH,
        )
        copy.start()
        sq_copies.append(copy)
        copy = pltpu.make_async_remote_copy(
            src_ref=ends.at[m], dst_ref=ends.at[m],
            send_sem=q_ss.at[3 + n], recv_sem=q_rs.at[3 + n],
            device_id=peer, device_id_type=MESH,
        )
        copy.start()
        sq_copies.append(copy)
    for a in range(4):
        for e in range(3):
            out_x[e, :, HALF * a : HALF * (a + 1)] = wide[3 + e][2 * a : 2 * a + 2]
    for copy in sq_copies:
        copy.wait()
    for n in range(SIDE):
        for e in range(3):
            for a in range(4):
                lo = 512 * n + HALF * a
                out_bc[e, :, lo : lo + HALF] = ends[n, e, 2 * a : 2 * a + 2, :]
    total = sqsend[...] + sqrecv[0] + sqrecv[1] + sqrecv[2]
    even = lax.broadcasted_iota(jnp.int32, (8, HALF), 0) % 2 == 0
    gains = jnp.concatenate([gain[n // 2 : n // 2 + 1, :] for n in range(8)], axis=0)
    for t in range(STEPS):
        col = jnp.sum(jnp.where(lane8 == t, total, 0.0), axis=1, keepdims=True)
        col = jnp.broadcast_to(col, (8, HALF))
        of_even = jnp.sum(jnp.where(even, col, 0.0), axis=0, keepdims=True)
        of_odd = jnp.sum(jnp.where(even, 0.0, col), axis=0, keepdims=True)
        factor = lax.rsqrt(jnp.where(even, of_even, of_odd) / NORM_WIDTH + 1e-05)
        on = jnp.where(even, active[0, t], active[1, t]) > 0
        normed = jnp.where(on, gated[t] * factor * gains, 0.0)
        for a in range(4):
            out_m[t, :, HALF * a : HALF * (a + 1)] = normed[2 * a : 2 * a + 2]

    for part in range(PARTS):
        own_finals[part].wait()
        for offset in OFFSETS:
            p = at(offset)[0]
            final_copy(p, part, p).wait_recv()
    for offset in OFFSETS:
        p, qq, cc = at(offset)
        small_copy(p, d).wait_send()
        read_copy(p, d).wait_send()
        for part in range(PARTS):
            state_copy(p, qq, cc, part, d).wait_send()
            final_copy(p, part, d).wait_send()


def finish(*refs):
    given, outs, held, mixer, sems = refs[:4], refs[4:8], refs[8:12], refs[12], refs[13]
    def ends(refs):
        return (refs[0].at[0], refs[0].at[1], *refs[1:])

    given, held, outs = ends(given), ends(held), ends(outs)
    loads = [
        pltpu.make_async_copy(source, target, sems.at[0, n])
        for n, (source, target) in enumerate(zip(given, held))
    ]
    for copy in loads:
        copy.start()
    stores = [
        pltpu.make_async_copy(source, target, sems.at[1, n])
        for n, (source, target) in enumerate(zip((*held[:4], mixer), outs))
    ]
    for n in (0, 1, 2, 3):
        loads[n].wait()
        stores[n].start()
    loads[4].wait()
    mixer[...] = held[4][...].astype(jnp.bfloat16)
    stores[4].start()
    for copy in stores:
        copy.wait()


def local(
    ssm_state, conv_x, conv_bc, x_in, bc_in, z_in, dt_in, conv_w_x, conv_w_bc,
    dt_bias, a_rate, d_skip, norm_gain, send_slot, dest_group, active,
):
    f32 = jnp.float32
    vmem = pl.BlockSpec(memory_space=pltpu.VMEM)
    hbm = pl.BlockSpec(memory_space=pltpu.HBM)
    dma = pltpu.SemaphoreType.DMA
    shapes = [
        jax.ShapeDtypeStruct((2, 512, 256), f32),
        jax.ShapeDtypeStruct((STEPS, 2, 512), f32),
        jax.ShapeDtypeStruct((3, 2, 512), f32),
        jax.ShapeDtypeStruct((3, 2, 2048), f32),
    ]
    state, mix, final_x, final_bc = pl.pallas_call(
        kernel,
        out_shape=tuple(shapes),
        in_specs=[hbm] * (1 + FIXED),
        out_specs=(hbm, vmem, vmem, vmem),
        scratch_shapes=[
            pltpu.VMEM((3, 2, 512), f32),
            pltpu.VMEM((STEPS, 2, 512), jnp.bfloat16),
            pltpu.VMEM((3, 2, 2048), f32),
            pltpu.VMEM((STEPS, 2, 2048), jnp.bfloat16),
            pltpu.VMEM((STEPS, 2, 512), jnp.bfloat16),
            pltpu.VMEM((STEPS, 2, 8), jnp.bfloat16),
            pltpu.VMEM((4, 512), f32),
            pltpu.VMEM((4, 2048), f32),
            pltpu.VMEM((4, HALF), f32),
            pltpu.VMEM((STEPS, PLANE), jnp.int32),
            pltpu.VMEM((STEPS, PLANE), jnp.int32),
            pltpu.SMEM((2, STEPS), jnp.int32),
            pltpu.SMEM((8,), f32),
            pltpu.SMEM((8,), f32),
            pltpu.SMEM((8,), f32),
            dma((16,)),
            pltpu.VMEM((PLANE, 4, 8, HALF), f32),
            pltpu.VMEM((4, PLANE * 8, HALF), f32),
            pltpu.VMEM((2, PLANE, PART, HALF), f32),
            pltpu.VMEM((2, PLANE, PART, HALF), f32),
            pltpu.VMEM((PARTS, 2, PLANE, PART, HALF), f32),
            pltpu.VMEM((STEPS, CHUNK, HALF), f32),
            pltpu.VMEM((STEPS, 8, HALF), f32),
            pltpu.VMEM((STEPS, 2, ROWS, HALF), f32),
            pltpu.VMEM((2, ROWS, HALF), f32),
            pltpu.VMEM((PLANE, 2, 256), f32),
            pltpu.VMEM((PLANE, 2, 256), f32),
            pltpu.VMEM((SIDE, 3, 8, HALF), f32),
            pltpu.VMEM((ROWS, STEPS, CHUNK, HALF), f32),
            pltpu.VMEM((ROWS, STEPS, 8, HALF), f32),
            pltpu.VMEM((8, HALF), f32),
            pltpu.VMEM((3, 8, HALF), f32),
            pltpu.VMEM((8, HALF), jnp.int32),
            pltpu.VMEM((STEPS, 2, 2048), f32),
            pltpu.VMEM((2, 4, 8, HALF), f32),
            pltpu.VMEM((8, HALF), f32),
            pltpu.SMEM((8, HALF), jnp.int32),
            dma((PLANE,)), dma((PLANE,)),
            dma((PARTS, PLANE)), dma((PARTS, PLANE)),
            dma((PARTS, PLANE)), dma((PARTS, PLANE)),
            dma((PLANE,)), dma((PLANE,)),
            dma((8,)), dma((8,)),
            dma((8,)),
        ],
        compiler_params=pltpu.CompilerParams(
            collective_id=0, has_side_effects=True, vmem_limit_bytes=VMEM_BYTES
        ),
    )(
        ssm_state.reshape(2, 512, 256), jnp.swapaxes(conv_x, 0, 1), x_in,
        jnp.swapaxes(conv_bc, 0, 1), bc_in, z_in, dt_in, conv_w_x, conv_w_bc,
        norm_gain.reshape(4, HALF), dest_group, send_slot, jnp.transpose(active),
        dt_bias, a_rate, d_skip,
    )
    bits = jax.ShapeDtypeStruct((STEPS, 2, 512), jnp.bfloat16)
    state, final_x, final_bc, mixer = pl.pallas_call(
        finish,
        out_shape=(shapes[0], shapes[2], shapes[3], bits),
        in_specs=[hbm] * 4,
        out_specs=(hbm,) * 4,
        scratch_shapes=[
            pltpu.VMEM(shapes[n].shape, f32) for n in (0, 2, 3, 1)
        ] + [pltpu.VMEM(bits.shape, jnp.bfloat16), dma((2, 5))],
        compiler_params=pltpu.CompilerParams(vmem_limit_bytes=VMEM_BYTES),
    )(state, final_x, final_bc, mix)
    return (
        mixer,
        state.reshape(ssm_state.shape),
        jnp.swapaxes(final_x, 0, 1),
        jnp.swapaxes(final_bc, 0, 1),
    )


def solution(mesh):
    return jax.shard_map(
        local,
        mesh=mesh,
        in_specs=(
            P("dp", "tensor", None, None),
            P("dp", None, "tensor"),
            P("dp", None, None),
            P(None, "dp", "tensor"),
            P(None, "dp", None),
            P(None, "dp", "tensor"),
            P(None, "dp", "tensor"),
            P(None, "tensor"),
            P(),
            P("tensor"),
            P("tensor"),
            P("tensor"),
            P("tensor"),
            P(),
            P(),
            P(None, "dp"),
        ),
        out_specs=(
            P(None, "dp", "tensor"),
            P("dp", "tensor", None, None),
            P("dp", None, "tensor"),
            P("dp", None, None),
        ),
        check_vma=False,
    )
```
